256 devices in a mesh: gx: 16 (over x_hi, z), gy: 8 (over y, core), ta: 2 (over x_lo).
Axes of the slice: x: 4 (x_hi: 2, x_lo: 2; x = x_hi * 2 + x_lo), y: 4, z: 8, core: 2. Of those that a mesh axis runs over, the one named last changes fastest.
Arguments:
- whitened: float32 [2, 512, 16384], P(None, 'gx', ('gy', 'ta')), may hold values from -6 to 6
- factor_x: float32 [512, 512], P('gx'), as said below
- factor_y: float32 [256, 256], P(('gy', 'ta')), as said below
- factor_t: float32 [64, 64], replicated, as said below
- mark_loadings: float32 [2, 64], replicated, may hold values from -1 to 1
- mark_offsets: float32 [64], replicated, may hold values from -1.5 to 1.5
- exposure: float32 [512, 16384], P('gx', ('gy', 'ta')), may hold values from 0.3 to 3
- counts: int32 [64, 512, 16384], P(None, 'gx', ('gy', 'ta')), may hold values from 0 to 3
Outputs:
- gradient: float32 [2, 512, 16384], P(None, 'gx', ('gy', 'ta'))
The draws below stay inside these ranges and needn't reach their ends.
Inputs may be any that keep to these rules, and one draw needn't show every extreme that they name: `factor_x`: A dense square matrix. `factor_y`: A dense square matrix. `factor_t`: A dense square matrix.
All inputs are finite; a program needn't handle non-finite values.
Results may differ from the reference program's by a relative error of at most 0.0003.
Values sent between devices are 32-bit elements; how exact they have to be, the bound alone decides.
A program may use at most 128 MiB of HBM per device.

```python
import math
import jax
import jax.numpy as jnp
from jax import lax

NX = 512
NY = 256
NT = 64
M = 64


def factor_table(key, order, smooth):
    places = jnp.arange(order).astype(jnp.float32)
    distance = jnp.abs(places[:, None] - places[None, :])
    noise = jnp.clip(jax.random.normal(key, (order, order), jnp.float32), -4.0, 4.0)
    reach = order * 0.5
    kernel = smooth * jnp.exp(-distance / reach) / jnp.sqrt(jnp.float32(reach))
    return jnp.eye(order, dtype=jnp.float32) + 0.6 * noise / jnp.sqrt(jnp.float32(order)) + kernel


def draw_factor_x(key, part):
    key = jax.random.fold_in(key, 11)
    smooth = 0.5
    return factor_table(key, NX, smooth)


def draw_factor_y(key, part):
    key = jax.random.fold_in(key, 23)
    smooth = 0.5
    return factor_table(key, NY, smooth)


def draw_factor_t(key, part):
    key = jax.random.fold_in(key, 37)
    smooth = 0.5
    return factor_table(key, NT, smooth)


def touch_ends(drawn, key, least, top_value):
    shape = drawn.shape
    place = [jax.random.randint(jax.random.fold_in(key, axis), (), 0, shape[axis]) for axis in range(len(shape))]
    drawn = drawn.at[tuple(place)].set(least)
    longest = shape.index(max(shape))
    place[longest] = (place[longest] + 1) % shape[longest]
    return drawn.at[tuple(place)].set(top_value)


def shard_levels(own_key, shape, shards, least, high):
    level, own = 1.0, jax.random.fold_in(own_key, 6)
    for axis_at, blocks in shards:
        steps = jnp.exp(jax.random.uniform(jax.random.fold_in(own, axis_at), (blocks,), jnp.float32, least / len(shards), high / len(shards)))
        level = level * jnp.repeat(steps, shape[axis_at] // blocks).reshape([-1 if axis == axis_at else 1 for axis in range(len(shape))])
    return level


def normal_values(rng, shape, deviation, most, shards=(), held_as=jnp.bfloat16):
    array = deviation * jax.random.normal(rng, shape, jnp.float32)
    if shards:
        array = array * shard_levels(rng, shape, shards, -0.22, 0.18)
    return jnp.clip(array, -most, most).astype(held_as)


def setup_inputs(seed: int = 0) -> dict:
    splits = jax.random.split(jax.random.key(seed), 9)
    return {
        "whitened": normal_values(splits[0], (2, NX, NY * NT), 1.0, 6.0, ((1, 16), (2, 16)), jnp.float32),
        "factor_x": draw_factor_x(jax.random.fold_in(splits[8], 71), 0),
        "factor_y": draw_factor_y(jax.random.fold_in(splits[8], 71), 0),
        "factor_t": draw_factor_t(jax.random.fold_in(splits[8], 71), 0),
        "mark_loadings": normal_values(splits[4], (2, M), 0.25, 1.0, (), jnp.float32),
        "mark_offsets": normal_values(splits[5], (M,), 0.5, 1.5, (), jnp.float32),
        "exposure": jnp.clip(jnp.exp(math.log(3.0) - 2.3025851 * jax.random.uniform(splits[6], (NX, NY * NT), jnp.float32) ** shard_levels(splits[6], (NX, NY * NT), ((0, 16), (1, 16)), -0.2, 0.2)), 0.3, 3.0),
        "counts": touch_ends(jax.random.randint(splits[7], (M, NX, NY * NT), 0, 4), jax.random.fold_in(splits[7], 1), 0, 3).astype(jnp.int32),
    }


def reference(whitened, factor_x, factor_y, factor_t, mark_loadings, mark_offsets, exposure, counts):
    highest = lax.Precision.HIGHEST
    latent = whitened.reshape(2, NX, NY, NT)
    rates = exposure.reshape(NX, NY, NT)
    events = counts.reshape(M, NX, NY, NT)
    field = jnp.einsum('ak,ckyt->cayt', factor_x, latent, precision=highest)
    field = jnp.einsum('bk,cxkt->cxbt', factor_y, field, precision=highest)
    field = jnp.einsum('sk,cxyk->cxys', factor_t, field, precision=highest)

    def one_mark(total, inputs):
        loadings, offset, mark_counts = inputs
        log_rate = offset + loadings[0] * field[0] + loadings[1] * field[1]
        residual = mark_counts.astype(jnp.float32) - rates * jnp.exp(log_rate)
        return total + loadings[:, None, None, None] * residual[None], None

    start = jnp.zeros(field.shape, jnp.float32)
    field_grad, _ = lax.scan(one_mark, start, (mark_loadings.T, mark_offsets, events))
    back = jnp.einsum('sk,cxys->cxyk', factor_t, field_grad, precision=highest)
    back = jnp.einsum('bk,cxbt->cxkt', factor_y, back, precision=highest)
    back = jnp.einsum('ak,cayt->ckyt', factor_x, back, precision=highest)
    return (back - latent).reshape(2, NX, NY * NT)
```

```python
import jax
import jax.numpy as jnp
from jax import lax
from jax.sharding import PartitionSpec as P

NT = 64
HIGHEST_PRECISION = lax.Precision.HIGHEST
YS = ("gy", "ta")


def x_mix(field, matrix):
    moved = lax.all_to_all(field, "gx", split_axis=2, concat_axis=1, tiled=True)
    mixed = jnp.einsum("ak,ckz->caz", matrix, moved, precision=HIGHEST_PRECISION)
    return lax.all_to_all(mixed, "gx", split_axis=1, concat_axis=2, tiled=True)


def y_mix(field, matrix):
    moved = lax.all_to_all(field, YS, split_axis=1, concat_axis=2, tiled=True)
    lines = moved.shape[1]
    shaped = moved.reshape(2, lines, matrix.shape[0], NT)
    mixed = jnp.einsum("bk,cxkt->cxbt", matrix, shaped, precision=HIGHEST_PRECISION)
    mixed = mixed.reshape(2, lines, matrix.shape[0] * NT)
    return lax.all_to_all(mixed, YS, split_axis=2, concat_axis=1, tiled=True)


def time_mix(field, matrix):
    lines = field.shape[1]
    merged = field.shape[2]
    shaped = field.reshape(2, lines, merged // NT, NT)
    mixed = jnp.einsum("sk,cxyk->cxys", matrix, shaped, precision=HIGHEST_PRECISION)
    return mixed.reshape(2, lines, merged)


def body(whitened, factor_x, factor_y, factor_t, mark_loadings, mark_offsets, exposure, counts):
    full_x = lax.all_gather(factor_x, "gx", axis=0, tiled=True)
    full_y = lax.all_gather(factor_y, YS, axis=0, tiled=True)
    field = x_mix(whitened, full_x)
    field = y_mix(field, full_y)
    field = time_mix(field, factor_t)
    first = mark_loadings[0][:, None, None]
    second = mark_loadings[1][:, None, None]
    log_rate = mark_offsets[:, None, None] + first * field[0][None] + second * field[1][None]
    residual = counts.astype(jnp.float32) - exposure[None] * jnp.exp(log_rate)
    field_grad = jnp.einsum("cm,mxz->cxz", mark_loadings, residual, precision=HIGHEST_PRECISION)
    back = time_mix(field_grad, factor_t.T)
    back = y_mix(back, full_y.T)
    back = x_mix(back, full_x.T)
    return back - whitened


def solution(mesh):
    placed = (
        P(None, "gx", ("gy", "ta")),
        P("gx", None),
        P(("gy", "ta"), None),
        P(),
        P(),
        P(),
        P("gx", ("gy", "ta")),
        P(None, "gx", ("gy", "ta")),
    )
    return jax.shard_map(
        body, mesh=mesh, in_specs=placed, out_specs=P(None, "gx", ("gy", "ta")), check_vma=False
    )
```

```python
import functools
import math

import jax
import jax.numpy as jnp
from jax import lax
from jax.experimental import pallas as pl
from jax.experimental.pallas import tpu as pltpu
from jax.sharding import PartitionSpec as P

MESH = pl.DeviceIdType.MESH
HIGHEST = lax.Precision.HIGHEST
F32 = jnp.float32
LOG2E = math.log2(math.e)
N = 16
PIECE = 32
ROWS = N * PIECE
MARKS = 64
SHIFT = 8.0
Y_IN, Y_OUT, X_IN, X_OUT, BX_IN, BX_OUT, BY_IN, BY_OUT = range(8)


def dot(a, b, dims):
    return lax.dot_general(a, b, (dims, ((), ())), precision=HIGHEST, preferred_element_type=F32)


def kernel(
    load_ref, off_ref, w_hbm, fx_hbm, fy_hbm, kt_ref, exp_hbm, counts_hbm, out_ref,
    w_v, exp_v, counts_v, sums_v,
    fx_v, fxt_v, fy_v,
    t_v, send_v, recv_v,
    local_sem, send_sem, recv_sem, fx_sem, fy_sem,
):
    gx = lax.axis_index("gx")
    gy = lax.axis_index("gy")
    ta = lax.axis_index("ta")
    j = gy * 2 + ta
    core = lax.rem(gy, 2)

    def x_peer(d):
        k = lax.rem(gx + d, N)
        return k, {"gx": k}

    def y_peer(d):
        k = lax.rem(j + d, N)
        return k, {"gy": k // 2, "ta": lax.rem(k, 2)}

    load_w = pltpu.make_async_copy(w_hbm, w_v, local_sem.at[0])
    load_w.start()
    load_fx = pltpu.make_async_copy(fx_hbm.at[core], fx_v.at[gx, core], local_sem.at[1])
    load_fx.start()
    load_fy = pltpu.make_async_copy(fy_hbm, fy_v.at[:, j], local_sem.at[2])
    load_fy.start()
    load_exp = pltpu.make_async_copy(exp_hbm, exp_v, local_sem.at[3])
    load_exp.start()
    load_counts = pltpu.make_async_copy(counts_hbm, counts_v, local_sem.at[4])
    load_counts.start()

    barrier = pltpu.get_barrier_semaphore()

    def greet(d, carry):
        _, at = y_peer(d)
        pl.semaphore_signal(barrier, inc=1, device_id=at, device_id_type=MESH)
        _, at = x_peer(d)
        pl.semaphore_signal(barrier, inc=1, device_id=at, device_id_type=MESH)
        return carry

    lax.fori_loop(1, N, greet, 0)

    def rows_of(k):
        return pl.ds(pl.multiple_of(k * PIECE, PIECE), PIECE)

    def exchange(phase, me, peer):
        recv_v[phase, rows_of(me), :] = send_v[phase, rows_of(me), :]

        def one(d, carry):
            k, at = peer(d)
            pltpu.make_async_remote_copy(
                src_ref=send_v.at[phase, rows_of(k)],
                dst_ref=recv_v.at[phase, rows_of(me)],
                send_sem=send_sem.at[phase],
                recv_sem=recv_sem.at[phase],
                device_id=at,
                device_id_type=MESH,
            ).start()
            return carry

        lax.fori_loop(1, N, one, 0)

    def arrived(phase):
        part = recv_v.at[phase, pl.ds(0, ROWS - PIECE)]
        pltpu.make_async_copy(part, part, recv_sem.at[phase]).wait()

    def sent(phase):
        part = send_v.at[phase, pl.ds(0, ROWS - PIECE)]
        pltpu.make_async_copy(part, part, send_sem.at[phase]).wait()

    def lines_to_columns(src, phase):
        for c in range(2):
            for x in range(32):
                send_v[phase, pl.ds((c * 32 + x) * 8, 8), :] = src[pl.ds(c * 256 + x, 8, stride=32), :]

    low = lax.broadcasted_iota(jnp.int32, (128, 128), 1) < 64

    def y_mix(source, target, dims):
        packed = []
        for pair in range(2):
            first = jnp.concatenate([recv_v[source, pl.ds(k * PIECE + pair * 16, 8), :] for k in range(N)], axis=0)
            second = jnp.concatenate([recv_v[source, pl.ds(k * PIECE + pair * 16 + 8, 8), :] for k in range(N)], axis=0)
            even = jnp.where(low, first, pltpu.roll(second, 64, 1))
            odd = jnp.where(low, pltpu.roll(first, 64, 1), second)
            packed.append(jnp.concatenate([even, odd], axis=0))
        matrix = fy_v[...].reshape(256, 256)
        mixed = dot(matrix, jnp.concatenate(packed, axis=1), dims)
        for pair in range(2):
            even = mixed[:128, pair * 128 : pair * 128 + 128]
            odd = mixed[128:, pair * 128 : pair * 128 + 128]
            first = jnp.where(low, even, pltpu.roll(odd, 64, 1))
            second = jnp.where(low, pltpu.roll(even, 64, 1), odd)
            for k in range(N):
                send_v[target, pl.ds(k * PIECE + pair * 16, 8), :] = first[k * 8 : k * 8 + 8]
                send_v[target, pl.ds(k * PIECE + pair * 16 + 8, 8), :] = second[k * 8 : k * 8 + 8]

    def count_sums(begin, end):
        for xt in range(begin, end):
            xs = slice(xt * 8, xt * 8 + 8)

            def mark(m, acc):
                tile = counts_v[m, xs, :].astype(F32)
                return acc[0] + load_ref[0, m] * tile, acc[1] + load_ref[1, m] * tile

            zero = jnp.zeros((8, 1024), F32)
            first, second = lax.fori_loop(0, MARKS, mark, (zero, zero), unroll=2)
            sums_v[0, xs, :] = first
            sums_v[1, xs, :] = second

    load_w.wait()
    load_fx.wait()
    load_fy.wait()
    lines = jnp.concatenate([w_v[c, :, g * 128 : g * 128 + 128] for c in range(2) for g in range(8)], axis=0)
    t_v[...] = dot(lines, kt_ref[...], ((1,), (1,)))
    lines_to_columns(t_v, Y_IN)

    pl.semaphore_wait(barrier, 2 * (N - 1))

    exchange(Y_IN, j, y_peer)

    def send_fy(d, carry):
        _, at = y_peer(d)
        pltpu.make_async_remote_copy(
            src_ref=fy_v.at[:, j], dst_ref=fy_v.at[:, j], send_sem=fy_sem.at[0], recv_sem=fy_sem.at[1],
            device_id=at, device_id_type=MESH,
        ).start()
        return carry

    lax.fori_loop(1, N, send_fy, 0)

    def send_fx(d, carry):
        _, at = x_peer(d)
        pltpu.make_async_remote_copy(
            src_ref=fx_v.at[gx, core], dst_ref=fx_v.at[gx, core], send_sem=fx_sem.at[0], recv_sem=fx_sem.at[1],
            device_id=at, device_id_type=MESH,
        ).start()
        return carry

    lax.fori_loop(1, N, send_fx, 0)

    load_counts.wait()
    count_sums(0, 2)

    arrived(Y_IN)
    fy_part = fy_v.at[:, pl.ds(0, N - 1)]
    pltpu.make_async_copy(fy_part, fy_part, fy_sem.at[1]).wait()
    y_mix(Y_IN, Y_OUT, ((1,), (0,)))
    exchange(Y_OUT, j, y_peer)
    count_sums(2, 4)
    arrived(Y_OUT)

    def columns_to_lines(phase, c, g, xt):
        return recv_v[phase, pl.ds((c * 32 + xt * 8) * 8 + g, 8, stride=8), :]

    for c in range(2):
        for g in range(8):
            for xt in range(4):
                send_v[X_IN, pl.ds(c * 256 + g * 32 + xt * 8, 8), :] = columns_to_lines(Y_OUT, c, g, xt)
    exchange(X_IN, gx, x_peer)

    fx_part = fx_v.at[pl.ds(0, N - 1), 0]
    pltpu.make_async_copy(fx_part, fx_part, fx_sem.at[1]).wait()
    swap = pltpu.make_async_remote_copy(
        src_ref=fx_v.at[:, core], dst_ref=fx_v.at[:, core], send_sem=fx_sem.at[2], recv_sem=fx_sem.at[3],
        device_id={"gy": gy + 1 - 2 * core}, device_id_type=MESH,
    )
    swap.start()
    swap.wait()
    fxt_v[...] = jnp.transpose(fx_v[...].reshape(ROWS, ROWS))

    arrived(X_IN)
    send_v[X_OUT] = dot(fx_v[...].reshape(ROWS, ROWS), recv_v[X_IN], ((1,), (0,)))
    exchange(X_OUT, gx, x_peer)
    load_exp.wait()
    arrived(X_OUT)

    for c_g in range(8):
        f0 = recv_v[X_OUT, c_g * 32 : c_g * 32 + 32, :] * LOG2E
        f1 = recv_v[X_OUT, 256 + c_g * 32 : 256 + c_g * 32 + 32, :] * LOG2E

        def mark(m, acc):
            l0 = load_ref[0, m]
            l1 = load_ref[1, m]
            rate = jnp.exp2(l0 * f0 + (l1 * f1 + (off_ref[m] * LOG2E - SHIFT)))
            return acc[0] + l0 * rate, acc[1] + l1 * rate

        zero = jnp.zeros((32, 128), F32)
        a0, a1 = lax.fori_loop(0, MARKS, mark, (zero, zero), unroll=4)
        cols = slice(c_g * 128, c_g * 128 + 128)
        scale = exp_v[:, cols] * (2.0**SHIFT)
        t_v[c_g * 32 : c_g * 32 + 32, :] = sums_v[0, :, cols] - scale * a0
        t_v[256 + c_g * 32 : 256 + c_g * 32 + 32, :] = sums_v[1, :, cols] - scale * a1

    send_v[BX_IN] = dot(t_v[...], kt_ref[...], ((1,), (0,)))
    exchange(BX_IN, gx, x_peer)
    arrived(BX_IN)
    send_v[BX_OUT] = dot(fxt_v[...], recv_v[BX_IN], ((1,), (0,)))
    exchange(BX_OUT, gx, x_peer)
    arrived(BX_OUT)
    lines_to_columns(recv_v.at[BX_OUT], BY_IN)
    exchange(BY_IN, j, y_peer)
    arrived(BY_IN)
    y_mix(BY_IN, BY_OUT, ((0,), (0,)))
    exchange(BY_OUT, j, y_peer)
    arrived(BY_OUT)
    for c in range(2):
        for g in range(8):
            for xt in range(4):
                xs = slice(xt * 8, xt * 8 + 8)
                cols = slice(g * 128, g * 128 + 128)
                out_ref[c, xs, cols] = columns_to_lines(BY_OUT, c, g, xt) - w_v[c, xs, cols]

    for phase in range(8):
        sent(phase)
    pltpu.make_async_copy(fy_part, fy_part, fy_sem.at[0]).wait()
    pltpu.make_async_copy(fx_part, fx_part, fx_sem.at[0]).wait()


def body(whitened, factor_x, factor_y, factor_t, mark_loadings, mark_offsets, exposure, counts):
    nothing = jnp.zeros_like(factor_t)
    twice = jnp.block([[factor_t, nothing], [nothing, factor_t]])
    fy = factor_y.reshape(8, 2, 16, 8, 2).transpose(1, 0, 4, 2, 3).reshape(2, 8, 256)
    fx = factor_x.reshape(2, 16, 512)
    anywhere = pl.BlockSpec(memory_space=pl.ANY)
    smem = pl.BlockSpec(memory_space=pltpu.SMEM)
    vmem = pl.BlockSpec(memory_space=pltpu.VMEM)
    return pl.pallas_call(
        kernel,
        out_shape=jax.ShapeDtypeStruct((2, 32, 1024), F32),
        in_specs=[smem, smem, anywhere, anywhere, anywhere, vmem, anywhere, anywhere],
        out_specs=vmem,
        scratch_shapes=[
            pltpu.VMEM((2, 32, 1024), F32),
            pltpu.VMEM((32, 1024), F32),
            pltpu.VMEM((MARKS, 32, 1024), jnp.int32),
            pltpu.VMEM((2, 32, 1024), F32),
            pltpu.VMEM((N, 2, 16, 512), F32),
            pltpu.VMEM((512, 512), F32),
            pltpu.VMEM((2, N, 8, 256), F32),
            pltpu.VMEM((ROWS, 128), F32),
            pltpu.VMEM((8, ROWS, 128), F32),
            pltpu.VMEM((8, ROWS, 128), F32),
            pltpu.SemaphoreType.DMA((5,)),
            pltpu.SemaphoreType.DMA((8,)),
            pltpu.SemaphoreType.DMA((8,)),
            pltpu.SemaphoreType.DMA((4,)),
            pltpu.SemaphoreType.DMA((2,)),
        ],
        compiler_params=pltpu.CompilerParams(
            collective_id=0, has_side_effects=True, vmem_limit_bytes=40 * 1024 * 1024
        ),
    )(mark_loadings, mark_offsets, whitened, fx, fy, twice, exposure, counts)


def solution(mesh):
    placed = (
        P(None, "gx", ("gy", "ta")),
        P("gx", None),
        P(("gy", "ta"), None),
        P(),
        P(),
        P(),
        P("gx", ("gy", "ta")),
        P(None, "gx", ("gy", "ta")),
    )
    return jax.shard_map(
        body, mesh=mesh, in_specs=placed, out_specs=P(None, "gx", ("gy", "ta")), check_vma=False
    )
```

```python
import math

import jax
import jax.numpy as jnp
from jax import lax
from jax.experimental import pallas as pl
from jax.experimental.pallas import tpu as pltpu
from jax.sharding import PartitionSpec as P

MESH = pl.DeviceIdType.MESH
F32 = jnp.float32
BF16 = jnp.bfloat16
LOG2E = math.log2(math.e)
N = 16
PIECE = 32
ROWS = N * PIECE
MARKS = 64
SHIFT = 8.0
GROUP = 64
Y_IN, Y_OUT, X_IN, X_OUT, BY_IN, BY_OUT, SUMS = range(7)
X_STEPS = sorted(
    [(z, x) for z in range(8) for x in range(2) if z or x], key=lambda s: -(min(s[0], 8 - s[0]) + 2 * s[1])
)
Y_STEPS = sorted(
    [(y, c, x) for y in range(4) for c in range(2) for x in range(2) if y or c or x],
    key=lambda s: -(min(s[0], 4 - s[0]) + s[2]),
)


def split(a):
    high = a.astype(BF16)
    return high, (a - high.astype(F32)).astype(BF16)


def dot(a, b, dims=((1,), (0,))):
    def one(left, right):
        return lax.dot_general(left, right, (dims, ((), ())), preferred_element_type=F32)

    return one(a[0], b[0]) + (one(a[0], b[1]) + one(a[1], b[0]))


def swap_halves(a):
    return pltpu.roll(a, 64, 1)


def kernel(
    load_hbm, off_hbm, w_hbm, fx_hbm, fy_hbm, ft_hbm, exp_hbm, counts_hbm, out_ref,
    load_ref, off_ref, w_v, exp_v, counts_v, sums_v, ft_v,
    fx_v, fx_parts, fxt_parts, fy_v, fyt_parts,
    t_v, send_v, recv_v, exp_send, exp_recv,
    local_sem, send_sem, recv_sem, exp_sem, fx_sem, fy_sem,
):
    gx = lax.axis_index("gx")
    gy = lax.axis_index("gy")
    ta = lax.axis_index("ta")
    j = gy * 2 + ta
    core = lax.rem(gy, 2)

    def x_peer(step):
        x = gx // 8
        k = (x + step[1] - 2 * x * step[1]) * 8 + lax.rem(gx + step[0], 8)
        return k, {"gx": k}

    def y_peer(step):
        y = lax.rem(gy // 2 + step[0], 4)
        a = y * 2 + (core + step[1] - 2 * core * step[1])
        b = ta + step[2] - 2 * ta * step[2]
        return a * 2 + b, {"gy": a, "ta": b}

    x_peers = [x_peer(step) for step in X_STEPS]
    y_peers = [y_peer(step) for step in Y_STEPS]

    loads = []
    for number, (source, target) in enumerate(
        (
            (w_hbm, w_v),
            (ft_hbm, ft_v),
            (fy_hbm, fy_v.at[j]),
            (fx_hbm.at[core], fx_v.at[gx, core]),
            (load_hbm, load_ref),
            (off_hbm, off_ref),
            (exp_hbm, exp_v),
            (counts_hbm, counts_v),
        )
    ):
        loads.append(pltpu.make_async_copy(source, target, local_sem.at[number]))
        loads[-1].start()

    barrier = pltpu.get_barrier_semaphore()
    for _, at in y_peers + x_peers:
        pl.semaphore_signal(barrier, inc=1, device_id=at, device_id_type=MESH)

    def push(source, target, sends, receives, at):
        pltpu.make_async_remote_copy(
            src_ref=source, dst_ref=target, send_sem=sends, recv_sem=receives, device_id=at, device_id_type=MESH
        ).start()

    def rows_of(k, piece=PIECE):
        return pl.ds(pl.multiple_of(k * piece, piece), piece)

    def exchange(phase, me, peers):
        for k, at in peers:
            push(send_v.at[phase, rows_of(k)], recv_v.at[phase, rows_of(me)], send_sem.at[phase], recv_sem.at[phase], at)
        recv_v[phase, rows_of(me), :] = send_v[phase, rows_of(me), :]

    def bytes_of(part, sem):
        pltpu.make_async_copy(part, part, sem).wait()

    def arrived(phase):
        bytes_of(recv_v.at[phase, pl.ds(0, ROWS - PIECE)], recv_sem.at[phase])

    def sent(phase):
        bytes_of(send_v.at[phase, pl.ds(0, ROWS - PIECE)], send_sem.at[phase])

    def low(rows):
        return lax.broadcasted_iota(jnp.int32, (rows, 128), 1) < 64

    def pack(first, second):
        half = low(first.shape[0])
        return jnp.where(half, first, swap_halves(second)), jnp.where(half, swap_halves(first), second)

    def lines(ref):
        found = []
        for g in range(8):
            found += pack(ref[0, :, g * 128 : g * 128 + 128], ref[1, :, g * 128 : g * 128 + 128])
        return jnp.concatenate(found, axis=0)

    def lines_to_columns(load, phase):
        for x in range(32):
            send_v[phase, pl.ds(x * 16, 16), :] = load(pl.ds(x, 16, stride=32))

    def y_mix(source, target, matrix):
        both = [
            jnp.concatenate([recv_v[source, pl.ds(k * PIECE + h * 16, 16), :] for k in range(N)], axis=0)
            for h in range(2)
        ]
        mixed = dot(matrix, split(jnp.concatenate(both, axis=1)))
        for k in range(N):
            for h in range(2):
                send_v[target, pl.ds(k * PIECE + h * 16, 16), :] = mixed[k * 16 : k * 16 + 16, h * 128 : h * 128 + 128]

    def sum_counts():
        for xt in range(4):
            xs = slice(xt * 8, xt * 8 + 8)

            def mark(m, total):
                tile = counts_v[m, xs, :].astype(F32)
                return total[0] + load_ref[0, m] * tile, total[1] + load_ref[1, m] * tile

            zero = jnp.zeros((8, 1024), F32)
            sums_v[0, xs, :], sums_v[1, xs, :] = lax.fori_loop(0, MARKS, mark, (zero, zero), unroll=4)

    for number in range(4):
        loads[number].wait()
    nothing = jnp.zeros((64, 64), F32)
    time = split(
        jnp.concatenate(
            [jnp.concatenate([ft_v[...], nothing], axis=1), jnp.concatenate([nothing, ft_v[...]], axis=1)], axis=0
        )
    )
    t_v[...] = dot(split(lines(w_v)), time, ((1,), (1,)))
    lines_to_columns(lambda rows: t_v[rows, :], Y_IN)

    pl.semaphore_wait(barrier, 2 * (N - 1))

    for _, at in y_peers:
        push(fy_v.at[j], fy_v.at[j], fy_sem.at[0], fy_sem.at[1], at)
    exchange(Y_IN, j, y_peers)
    for _, at in x_peers:
        push(fx_v.at[gx, core], fx_v.at[gx, core], fx_sem.at[0], fx_sem.at[1], at)

    for number in range(4, 8):
        loads[number].wait()
    for g in range(8):
        cols = slice(g * 128, g * 128 + 128)
        even, odd = pack(exp_v[0:16, cols], exp_v[16:32, cols])
        exp_send[g * 32 : g * 32 + 16, :] = even
        exp_send[g * 32 + 16 : g * 32 + 32, :] = odd
    for k, at in x_peers:
        push(exp_send.at[rows_of(k, 16)], exp_recv.at[rows_of(gx, 16)], exp_sem.at[0], exp_sem.at[1], at)
    exp_recv[rows_of(gx, 16), :] = exp_send[rows_of(gx, 16), :]

    sum_counts()
    send_v[SUMS] = lines(sums_v)
    exchange(SUMS, gx, x_peers)

    fy_part = fy_v.at[pl.ds(0, N - 1)]
    bytes_of(fy_part, fy_sem.at[1])
    fy = fy_v[...].reshape(256, 256)
    arrived(Y_IN)
    y_mix(Y_IN, Y_OUT, split(fy))
    exchange(Y_OUT, j, y_peers)
    fyt_parts[0], fyt_parts[1] = split(jnp.transpose(fy))
    arrived(Y_OUT)

    for y in range(N):
        send_v[X_IN, pl.ds(y * 32, 32), :] = recv_v[Y_OUT, pl.ds(y, 32, stride=16), :]
    exchange(X_IN, gx, x_peers)

    fx_part = fx_v.at[pl.ds(0, N - 1), 0]
    bytes_of(fx_part, fx_sem.at[1])
    swap = pltpu.make_async_remote_copy(
        src_ref=fx_v.at[:, core], dst_ref=fx_v.at[:, core], send_sem=fx_sem.at[2], recv_sem=fx_sem.at[3],
        device_id={"gy": gy + 1 - 2 * core}, device_id_type=MESH,
    )
    swap.start()
    swap.wait()
    fx = fx_v[...].reshape(ROWS, ROWS)
    fx_parts[0], fx_parts[1] = split(fx)
    fxt_parts[0], fxt_parts[1] = split(jnp.transpose(fx))

    arrived(X_IN)
    t_v[...] = dot((fx_parts[0], fx_parts[1]), split(recv_v[X_IN]))
    bytes_of(exp_recv.at[pl.ds(0, (N - 1) * 16)], exp_sem.at[1])
    arrived(SUMS)

    for begin in range(0, 256, GROUP):
        firsts, seconds = [], []
        for k in range(begin // 16, (begin + GROUP) // 16):
            first, second = pack(t_v[k * 32 : k * 32 + 16, :], t_v[k * 32 + 16 : k * 32 + 32, :])
            firsts.append(first)
            seconds.append(second)
        f0 = jnp.concatenate(firsts, axis=0) * LOG2E
        f1 = jnp.concatenate(seconds, axis=0) * LOG2E

        def mark(m, total):
            l0 = load_ref[0, m]
            l1 = load_ref[1, m]
            rate = jnp.exp2(l0 * f0 + (l1 * f1 + (off_ref[m] * LOG2E - SHIFT)))
            return total[0] + l0 * rate, total[1] + l1 * rate

        zero = jnp.zeros((GROUP, 128), F32)
        a0, a1 = lax.fori_loop(0, MARKS, mark, (zero, zero), unroll=4)
        scale = exp_recv[begin : begin + GROUP, :] * (2.0**SHIFT)
        upper, lower = pack(scale * a0, scale * a1)
        for n in range(GROUP // 16):
            k = begin // 16 + n
            t_v[k * 32 : k * 32 + 16, :] = recv_v[SUMS, k * 32 : k * 32 + 16, :] - upper[n * 16 : n * 16 + 16]
            t_v[k * 32 + 16 : k * 32 + 32, :] = recv_v[SUMS, k * 32 + 16 : k * 32 + 32, :] - lower[n * 16 : n * 16 + 16]

    back = dot(split(t_v[...]), time)
    send_v[X_OUT] = dot((fxt_parts[0], fxt_parts[1]), split(back))
    exchange(X_OUT, gx, x_peers)
    arrived(X_OUT)
    lines_to_columns(lambda rows: recv_v[X_OUT, rows, :], BY_IN)
    exchange(BY_IN, j, y_peers)
    arrived(BY_IN)
    y_mix(BY_IN, BY_OUT, (fyt_parts[0], fyt_parts[1]))
    exchange(BY_OUT, j, y_peers)
    arrived(BY_OUT)
    for g in range(8):
        cols = slice(g * 128, g * 128 + 128)
        first, second = pack(
            recv_v[BY_OUT, pl.ds(2 * g, 32, stride=16), :], recv_v[BY_OUT, pl.ds(2 * g + 1, 32, stride=16), :]
        )
        out_ref[0, :, cols] = first - w_v[0, :, cols]
        out_ref[1, :, cols] = second - w_v[1, :, cols]

    for phase in range(7):
        sent(phase)
    bytes_of(exp_send.at[pl.ds(0, (N - 1) * 16)], exp_sem.at[0])
    bytes_of(fy_part, fy_sem.at[0])
    bytes_of(fx_part, fx_sem.at[0])


def body(whitened, factor_x, factor_y, factor_t, mark_loadings, mark_offsets, exposure, counts):
    fx = factor_x.reshape(2, 16, 512)
    return pl.pallas_call(
        kernel,
        out_shape=jax.ShapeDtypeStruct((2, 32, 1024), F32),
        in_specs=[pl.BlockSpec(memory_space=pltpu.HBM)] * 8,
        out_specs=pl.BlockSpec(memory_space=pltpu.VMEM),
        scratch_shapes=[
            pltpu.SMEM((2, MARKS), F32),
            pltpu.SMEM((MARKS,), F32),
            pltpu.VMEM((2, 32, 1024), F32),
            pltpu.VMEM((32, 1024), F32),
            pltpu.VMEM((MARKS, 32, 1024), jnp.int32),
            pltpu.VMEM((2, 32, 1024), F32),
            pltpu.VMEM((64, 64), F32),
            pltpu.VMEM((N, 2, 16, 512), F32),
            pltpu.VMEM((2, 512, 512), BF16),
            pltpu.VMEM((2, 512, 512), BF16),
            pltpu.VMEM((N, 16, 256), F32),
            pltpu.VMEM((2, 256, 256), BF16),
            pltpu.VMEM((ROWS, 128), F32),
            pltpu.VMEM((7, ROWS, 128), F32),
            pltpu.VMEM((7, ROWS, 128), F32),
            pltpu.VMEM((256, 128), F32),
            pltpu.VMEM((256, 128), F32),
            pltpu.SemaphoreType.DMA((8,)),
            pltpu.SemaphoreType.DMA((7,)),
            pltpu.SemaphoreType.DMA((7,)),
            pltpu.SemaphoreType.DMA((2,)),
            pltpu.SemaphoreType.DMA((4,)),
            pltpu.SemaphoreType.DMA((2,)),
        ],
        compiler_params=pltpu.CompilerParams(
            collective_id=0, has_side_effects=True, vmem_limit_bytes=60 * 1024 * 1024
        ),
    )(mark_loadings, mark_offsets, whitened, fx, factor_y, factor_t, exposure, counts)


def solution(mesh):
    placed = (
        P(None, "gx", ("gy", "ta")),
        P("gx", None),
        P(("gy", "ta"), None),
        P(),
        P(),
        P(),
        P("gx", ("gy", "ta")),
        P(None, "gx", ("gy", "ta")),
    )
    return jax.shard_map(
        body, mesh=mesh, in_specs=placed, out_specs=P(None, "gx", ("gy", "ta")), check_vma=False
    )
```

```python
import math

import jax
import jax.numpy as jnp
from jax import lax
from jax.experimental import pallas as pl
from jax.experimental.pallas import tpu as pltpu
from jax.sharding import PartitionSpec as P

MESH = pl.DeviceIdType.MESH
F32 = jnp.float32
BF16 = jnp.bfloat16
LOG2E = math.log2(math.e)
N = 16
PIECE = 32
ROWS = N * PIECE
MARKS = 64
SHIFT = 8.0
GROUP = 64
Y_IN, Y_OUT, X_IN, X_OUT, BY_IN, BY_OUT, SUMS = range(7)
X_STEPS = sorted(
    [(z, x) for z in range(8) for x in range(2) if z or x], key=lambda s: -(min(s[0], 8 - s[0]) + 2 * s[1])
)
Y_STEPS = sorted(
    [(y, c, x) for y in range(4) for c in range(2) for x in range(2) if y or c or x],
    key=lambda s: -(min(s[0], 4 - s[0]) + s[2]),
)


def split(a):
    high = a.astype(BF16)
    return high, (a - high.astype(F32)).astype(BF16)


def dot(a, b, dims=((1,), (0,))):
    def one(left, right):
        return lax.dot_general(left, right, (dims, ((), ())), preferred_element_type=F32)

    return one(a[0], b[0]) + (one(a[0], b[1]) + one(a[1], b[0]))


def swap_halves(a):
    return pltpu.roll(a, 64, 1)


def kernel(
    load_hbm, off_hbm, w_hbm, fx_hbm, fy_hbm, ft_hbm, exp_hbm, counts_hbm, out_ref,
    load_ref, off_ref, w_v, exp_v, counts_v, sums_v, ft_v,
    fx_v, fx_parts, fxt_parts, fy_v, fyt_parts,
    t_v, send_v, recv_v, exp_send, exp_recv,
    local_sem, send_sem, recv_sem, exp_sem, fx_sem, fy_sem,
):
    gx = lax.axis_index("gx")
    gy = lax.axis_index("gy")
    ta = lax.axis_index("ta")
    j = gy * 2 + ta
    core = lax.rem(gy, 2)
    row = gy // 2

    def x_peer(step):
        x = gx // 8
        k = (x + step[1] - 2 * x * step[1]) * 8 + lax.rem(gx + step[0], 8)
        return k, {"gx": k}

    def y_peer(step):
        y = lax.rem(gy // 2 + step[0], 4)
        a = y * 2 + (core + step[1] - 2 * core * step[1])
        b = ta + step[2] - 2 * ta * step[2]
        return a * 2 + b, {"gy": a, "ta": b}

    x_peers = [x_peer(step) for step in X_STEPS]
    y_peers = [y_peer(step) for step in Y_STEPS]

    loads = []
    for number, (source, target) in enumerate(
        (
            (w_hbm, w_v),
            (ft_hbm, ft_v),
            (fy_hbm, fy_v.at[row, core, ta]),
            (
                fx_hbm.at[pl.ds(pl.multiple_of(row * 8, 8), 8), pl.ds(pl.multiple_of(core * 256, 256), 256)],
                fx_v.at[core, gx, row],
            ),
            (load_hbm, load_ref),
            (off_hbm, off_ref),
            (exp_hbm, exp_v),
            (counts_hbm, counts_v),
        )
    ):
        loads.append(pltpu.make_async_copy(source, target, local_sem.at[number]))
        loads[-1].start()

    barrier = pltpu.get_barrier_semaphore()
    for _, at in y_peers + x_peers:
        pl.semaphore_signal(barrier, inc=1, device_id=at, device_id_type=MESH)

    def push(source, target, sends, receives, at):
        pltpu.make_async_remote_copy(
            src_ref=source, dst_ref=target, send_sem=sends, recv_sem=receives, device_id=at, device_id_type=MESH
        ).start()

    def rows_of(k, piece=PIECE):
        return pl.ds(pl.multiple_of(k * piece, piece), piece)

    def exchange(phase, me, peers):
        for k, at in peers:
            push(send_v.at[phase, rows_of(k)], recv_v.at[phase, rows_of(me)], send_sem.at[phase], recv_sem.at[phase], at)
        recv_v[phase, rows_of(me), :] = send_v[phase, rows_of(me), :]

    def bytes_of(part, sem):
        pltpu.make_async_copy(part, part, sem).wait()

    def arrived(phase):
        bytes_of(recv_v.at[phase, pl.ds(0, ROWS - PIECE)], recv_sem.at[phase])

    def sent(phase):
        bytes_of(send_v.at[phase, pl.ds(0, ROWS - PIECE)], send_sem.at[phase])

    def low(rows):
        return lax.broadcasted_iota(jnp.int32, (rows, 128), 1) < 64

    def pack(first, second):
        half = low(first.shape[0])
        return jnp.where(half, first, swap_halves(second)), jnp.where(half, swap_halves(first), second)

    def lines(ref):
        found = []
        for g in range(8):
            found += pack(ref[0, :, g * 128 : g * 128 + 128], ref[1, :, g * 128 : g * 128 + 128])
        return jnp.concatenate(found, axis=0)

    def lines_to_columns(load, phase):
        for x in range(32):
            send_v[phase, pl.ds(x * 16, 16), :] = load(pl.ds(x, 16, stride=32))

    def y_mix(source, target, matrix):
        both = [
            jnp.concatenate([recv_v[source, pl.ds(k * PIECE + h * 16, 16), :] for k in range(N)], axis=0)
            for h in range(2)
        ]
        mixed = dot(matrix, split(jnp.concatenate(both, axis=1)))
        for k in range(N):
            for h in range(2):
                send_v[target, pl.ds(k * PIECE + h * 16, 16), :] = mixed[k * 16 : k * 16 + 16, h * 128 : h * 128 + 128]

    def sum_counts():
        for xt in range(4):
            xs = slice(xt * 8, xt * 8 + 8)

            def mark(m, total):
                tile = counts_v[m, xs, :].astype(F32)
                return total[0] + load_ref[0, m] * tile, total[1] + load_ref[1, m] * tile

            zero = jnp.zeros((8, 1024), F32)
            sums_v[0, xs, :], sums_v[1, xs, :] = lax.fori_loop(0, MARKS, mark, (zero, zero), unroll=4)

    for number in range(4):
        loads[number].wait()
    nothing = jnp.zeros((64, 64), F32)
    time = split(
        jnp.concatenate(
            [jnp.concatenate([ft_v[...], nothing], axis=1), jnp.concatenate([nothing, ft_v[...]], axis=1)], axis=0
        )
    )
    t_v[...] = dot(split(lines(w_v)), time, ((1,), (1,)))
    lines_to_columns(lambda rows: t_v[rows, :], Y_IN)

    pl.semaphore_wait(barrier, 2 * (N - 1))

    mine = fy_v.at[row, core, ta]
    for step, (_, at) in zip(Y_STEPS, y_peers):
        if step[1] == 0:
            push(mine, mine, fy_sem.at[0], fy_sem.at[1], at)
    exchange(Y_IN, j, y_peers)
    for _, at in x_peers:
        push(fx_v.at[core, gx, row], fx_v.at[core, gx, row], fx_sem.at[0], fx_sem.at[1], at)

    for number in range(4, 8):
        loads[number].wait()
    for g in range(8):
        cols = slice(g * 128, g * 128 + 128)
        even, odd = pack(exp_v[0:16, cols], exp_v[16:32, cols])
        exp_send[g * 32 : g * 32 + 16, :] = even
        exp_send[g * 32 + 16 : g * 32 + 32, :] = odd
    for k, at in x_peers:
        push(exp_send.at[rows_of(k, 16)], exp_recv.at[rows_of(gx, 16)], exp_sem.at[0], exp_sem.at[1], at)
    exp_recv[rows_of(gx, 16), :] = exp_send[rows_of(gx, 16), :]

    sum_counts()
    send_v[SUMS] = lines(sums_v)
    exchange(SUMS, gx, x_peers)

    other = {"gy": gy + 1 - 2 * core}
    fy_half = fy_v.at[:, core]
    fy_part = recv_v.at[Y_IN, pl.ds(0, 7 * PIECE)]
    bytes_of(fy_part, fy_sem.at[1])
    push(fy_half, fy_half, fy_sem.at[2], fy_sem.at[3], other)
    arrived(Y_IN)
    bytes_of(fy_half, fy_sem.at[3])
    fy = fy_v[...].reshape(256, 256)
    y_mix(Y_IN, Y_OUT, split(fy))
    exchange(Y_OUT, j, y_peers)

    fx_eighth = fx_v.at[0, pl.ds(0, N - 1), 0]
    bytes_of(fx_eighth, fx_sem.at[1])
    for step in (2, 1, 3):
        at = {"gy": lax.rem(row + step, 4) * 2 + core}
        push(fx_v.at[core, :, row], fx_v.at[core, :, row], fx_sem.at[2], fx_sem.at[3], at)
    fyt_parts[0], fyt_parts[1] = split(jnp.transpose(fy))
    arrived(Y_OUT)

    for y in range(N):
        send_v[X_IN, pl.ds(y * 32, 32), :] = recv_v[Y_OUT, pl.ds(y, 32, stride=16), :]
    exchange(X_IN, gx, x_peers)

    fx_half = fx_v.at[0, :, pl.ds(0, 3)]
    bytes_of(fx_half, fx_sem.at[3])
    push(fx_v.at[core], fx_v.at[core], fx_sem.at[4], fx_sem.at[5], other)
    bytes_of(fx_v.at[0], fx_sem.at[5])
    fx = jnp.concatenate([fx_v[0].reshape(ROWS, 256), fx_v[1].reshape(ROWS, 256)], axis=1)
    fx_parts[0], fx_parts[1] = split(fx)
    fxt_parts[0], fxt_parts[1] = split(jnp.transpose(fx))

    arrived(X_IN)
    t_v[...] = dot((fx_parts[0], fx_parts[1]), split(recv_v[X_IN]))
    bytes_of(exp_recv.at[pl.ds(0, (N - 1) * 16)], exp_sem.at[1])
    arrived(SUMS)

    for begin in range(0, 256, GROUP):
        firsts, seconds = [], []
        for k in range(begin // 16, (begin + GROUP) // 16):
            first, second = pack(t_v[k * 32 : k * 32 + 16, :], t_v[k * 32 + 16 : k * 32 + 32, :])
            firsts.append(first)
            seconds.append(second)
        f0 = jnp.concatenate(firsts, axis=0) * LOG2E
        f1 = jnp.concatenate(seconds, axis=0) * LOG2E

        def mark(m, total):
            l0 = load_ref[0, m]
            l1 = load_ref[1, m]
            rate = jnp.exp2(l0 * f0 + (l1 * f1 + (off_ref[m] * LOG2E - SHIFT)))
            return total[0] + l0 * rate, total[1] + l1 * rate

        zero = jnp.zeros((GROUP, 128), F32)
        a0, a1 = lax.fori_loop(0, MARKS, mark, (zero, zero), unroll=4)
        scale = exp_recv[begin : begin + GROUP, :] * (2.0**SHIFT)
        upper, lower = pack(scale * a0, scale * a1)
        for n in range(GROUP // 16):
            k = begin // 16 + n
            t_v[k * 32 : k * 32 + 16, :] = recv_v[SUMS, k * 32 : k * 32 + 16, :] - upper[n * 16 : n * 16 + 16]
            t_v[k * 32 + 16 : k * 32 + 32, :] = recv_v[SUMS, k * 32 + 16 : k * 32 + 32, :] - lower[n * 16 : n * 16 + 16]

    back = dot(split(t_v[...]), time)
    send_v[X_OUT] = dot((fxt_parts[0], fxt_parts[1]), split(back))
    exchange(X_OUT, gx, x_peers)
    arrived(X_OUT)
    lines_to_columns(lambda rows: recv_v[X_OUT, rows, :], BY_IN)
    exchange(BY_IN, j, y_peers)
    arrived(BY_IN)
    y_mix(BY_IN, BY_OUT, (fyt_parts[0], fyt_parts[1]))
    exchange(BY_OUT, j, y_peers)
    arrived(BY_OUT)
    for g in range(8):
        cols = slice(g * 128, g * 128 + 128)
        first, second = pack(
            recv_v[BY_OUT, pl.ds(2 * g, 32, stride=16), :], recv_v[BY_OUT, pl.ds(2 * g + 1, 32, stride=16), :]
        )
        out_ref[0, :, cols] = first
        out_ref[1, :, cols] = second

    for phase in range(7):
        sent(phase)
    bytes_of(exp_send.at[pl.ds(0, (N - 1) * 16)], exp_sem.at[0])
    bytes_of(fy_part, fy_sem.at[0])
    bytes_of(fy_half, fy_sem.at[2])
    bytes_of(fx_eighth, fx_sem.at[0])
    bytes_of(fx_half, fx_sem.at[2])
    bytes_of(fx_v.at[0], fx_sem.at[4])


def body(whitened, factor_x, factor_y, factor_t, mark_loadings, mark_offsets, exposure, counts):
    back = pl.pallas_call(
        kernel,
        out_shape=jax.ShapeDtypeStruct((2, 32, 1024), F32),
        in_specs=[pl.BlockSpec(memory_space=pltpu.HBM)] * 8,
        out_specs=pl.BlockSpec(memory_space=pltpu.VMEM),
        scratch_shapes=[
            pltpu.SMEM((2, MARKS), F32),
            pltpu.SMEM((MARKS,), F32),
            pltpu.VMEM((2, 32, 1024), F32),
            pltpu.VMEM((32, 1024), F32),
            pltpu.VMEM((MARKS, 32, 1024), jnp.int32),
            pltpu.VMEM((2, 32, 1024), F32),
            pltpu.VMEM((64, 64), F32),
            pltpu.VMEM((2, N, 4, 8, 256), F32),
            pltpu.VMEM((2, 512, 512), BF16),
            pltpu.VMEM((2, 512, 512), BF16),
            pltpu.VMEM((4, 2, 2, 16, 256), F32),
            pltpu.VMEM((2, 256, 256), BF16),
            pltpu.VMEM((ROWS, 128), F32),
            pltpu.VMEM((7, ROWS, 128), F32),
            pltpu.VMEM((7, ROWS, 128), F32),
            pltpu.VMEM((256, 128), F32),
            pltpu.VMEM((256, 128), F32),
            pltpu.SemaphoreType.DMA((8,)),
            pltpu.SemaphoreType.DMA((7,)),
            pltpu.SemaphoreType.DMA((7,)),
            pltpu.SemaphoreType.DMA((2,)),
            pltpu.SemaphoreType.DMA((6,)),
            pltpu.SemaphoreType.DMA((4,)),
        ],
        compiler_params=pltpu.CompilerParams(
            collective_id=0, has_side_effects=True, vmem_limit_bytes=60 * 1024 * 1024
        ),
    )(mark_loadings, mark_offsets, whitened, factor_x, factor_y, factor_t, exposure, counts)
    return back - whitened


def solution(mesh):
    placed = (
        P(None, "gx", ("gy", "ta")),
        P("gx", None),
        P(("gy", "ta"), None),
        P(),
        P(),
        P(),
        P("gx", ("gy", "ta")),
        P(None, "gx", ("gy", "ta")),
    )
    return jax.shard_map(
        body, mesh=mesh, in_specs=placed, out_specs=P(None, "gx", ("gy", "ta")), check_vma=False
    )
```

```python
import math

import jax
import jax.numpy as jnp
from jax import lax
from jax.experimental import pallas as pl
from jax.experimental.pallas import tpu as pltpu
from jax.sharding import PartitionSpec as P

MESH = pl.DeviceIdType.MESH
F32 = jnp.float32
BF16 = jnp.bfloat16
LOG2E = math.log2(math.e)
N = 16
PIECE = 16
HALF = N * PIECE
ROWS = 2 * HALF
MARKS = 64
SHIFT = 8.0
GROUP = 64
Y_IN, Y_OUT, X_IN, X_OUT, BY_IN, BY_OUT, SUMS = range(7)
X_STEPS = sorted(
    [(z, x) for z in range(8) for x in range(2) if z or x], key=lambda s: -(min(s[0], 8 - s[0]) + 2 * s[1])
)
Y_STEPS = sorted(
    [(y, c, x) for y in range(4) for c in range(2) for x in range(2) if y or c or x],
    key=lambda s: -(min(s[0], 4 - s[0]) + s[2]),
)


def split(a):
    high = a.astype(BF16)
    return high, (a - high.astype(F32)).astype(BF16)


def dot(a, b, dims=((1,), (0,))):
    def one(left, right):
        return lax.dot_general(left, right, (dims, ((), ())), preferred_element_type=F32)

    return one(a[0], b[0]) + (one(a[0], b[1]) + one(a[1], b[0]))


def dot_wide(a, b):
    both = jnp.dot(a[0], jnp.concatenate([b[0], b[1]], axis=1), preferred_element_type=F32)
    return both[:, :128] + (both[:, 128:] + jnp.dot(a[1], b[0], preferred_element_type=F32))


def swap_halves(a):
    return pltpu.roll(a, 64, 1)


def kernel(
    load_hbm, off_hbm, w_hbm, fx_hbm, fy_hbm, ft_hbm, exp_hbm, counts_hbm, out_ref,
    load_ref, off_ref, w_v, exp_v, counts_v, sums_v, ft_v,
    fx_v, fx_parts, fxt_parts, fy_v, fyt_parts,
    t_v, field_v, send_v, recv_v, exp_send, exp_recv,
    local_sem, send_sem, recv_sem, sums_sem, exp_sem, fx_sem, fy_sem,
):
    gx = lax.axis_index("gx")
    gy = lax.axis_index("gy")
    ta = lax.axis_index("ta")
    j = gy * 2 + ta
    core = lax.rem(gy, 2)
    row = gy // 2

    def x_peer(step):
        x = gx // 8
        k = (x + step[1] - 2 * x * step[1]) * 8 + lax.rem(gx + step[0], 8)
        return k, {"gx": k}

    def y_peer(step):
        y = lax.rem(gy // 2 + step[0], 4)
        a = y * 2 + (core + step[1] - 2 * core * step[1])
        b = ta + step[2] - 2 * ta * step[2]
        return a * 2 + b, {"gy": a, "ta": b}

    x_peers = [x_peer(step) for step in X_STEPS]
    y_peers = [y_peer(step) for step in Y_STEPS]

    loads = []
    for number, (source, target) in enumerate(
        (
            (w_hbm, w_v),
            (ft_hbm, ft_v),
            (fy_hbm, fy_v.at[row, core, ta]),
            (
                fx_hbm.at[pl.ds(pl.multiple_of(row * 8, 8), 8), pl.ds(pl.multiple_of(core * 256, 256), 256)],
                fx_v.at[core, gx, row],
            ),
            (load_hbm, load_ref),
            (off_hbm, off_ref),
            (exp_hbm, exp_v),
            (counts_hbm, counts_v),
        )
    ):
        loads.append(pltpu.make_async_copy(source, target, local_sem.at[number]))
        loads[-1].start()

    barrier = pltpu.get_barrier_semaphore()
    for _, at in y_peers + x_peers:
        pl.semaphore_signal(barrier, inc=1, device_id=at, device_id_type=MESH)

    def push(source, target, sends, receives, at):
        pltpu.make_async_remote_copy(
            src_ref=source, dst_ref=target, send_sem=sends, recv_sem=receives, device_id=at, device_id_type=MESH
        ).start()

    def rows_of(k, piece, base=0):
        return pl.ds(pl.multiple_of(base + k * piece, piece), piece)

    def exchange(phase, half, me, peers):
        mine = rows_of(me, PIECE, half * HALF)
        for k, at in peers:
            push(
                send_v.at[phase, rows_of(k, PIECE, half * HALF)],
                recv_v.at[phase, mine],
                send_sem.at[phase, half],
                recv_sem.at[phase, half],
                at,
            )
        recv_v[phase, mine, :] = send_v[phase, mine, :]

    def bytes_of(part, sem):
        pltpu.make_async_copy(part, part, sem).wait()

    def arrived(phase, half):
        bytes_of(recv_v.at[phase, pl.ds(0, HALF - PIECE)], recv_sem.at[phase, half])

    def sent(phase, half):
        bytes_of(send_v.at[phase, pl.ds(0, HALF - PIECE)], send_sem.at[phase, half])

    def low(rows):
        return lax.broadcasted_iota(jnp.int32, (rows, 128), 1) < 64

    def pack(first, second):
        half = low(first.shape[0])
        return jnp.where(half, first, swap_halves(second)), jnp.where(half, swap_halves(first), second)

    def lines(ref):
        found = []
        for g in range(8):
            found += pack(ref[0, :, g * 128 : g * 128 + 128], ref[1, :, g * 128 : g * 128 + 128])
        return jnp.concatenate(found, axis=0)

    def turn(load, phase, half):
        for n in range(N):
            send_v[phase, pl.ds(half * HALF + n * N, N), :] = load(n)

    def y_mix(source, target, half, matrix):
        rows = pl.ds(half * HALF, HALF)
        send_v[target, rows, :] = dot_wide(matrix, split(recv_v[source, rows, :]))

    def sum_counts():
        for xt in range(4):
            xs = slice(xt * 8, xt * 8 + 8)

            def mark(m, total):
                tile = counts_v[m, xs, :].astype(F32)
                return total[0] + load_ref[0, m] * tile, total[1] + load_ref[1, m] * tile

            zero = jnp.zeros((8, 1024), F32)
            sums_v[0, xs, :], sums_v[1, xs, :] = lax.fori_loop(0, MARKS, mark, (zero, zero), unroll=4)

    for number in range(4):
        loads[number].wait()
    nothing = jnp.zeros((64, 64), F32)
    time = split(
        jnp.concatenate(
            [jnp.concatenate([ft_v[...], nothing], axis=1), jnp.concatenate([nothing, ft_v[...]], axis=1)], axis=0
        )
    )
    t_v[...] = dot(split(lines(w_v)), time, ((1,), (1,)))
    for half in range(2):
        turn(lambda n: t_v[pl.ds(half * N + n, N, stride=32), :], Y_IN, half)

    pl.semaphore_wait(barrier, 2 * (N - 1))

    mine = fy_v.at[row, core, ta]
    for step, (_, at) in zip(Y_STEPS, y_peers):
        if step[1] == 0:
            push(mine, mine, fy_sem.at[0], fy_sem.at[1], at)
    for half in range(2):
        exchange(Y_IN, half, j, y_peers)
    for _, at in x_peers:
        push(fx_v.at[core, gx, row], fx_v.at[core, gx, row], fx_sem.at[0], fx_sem.at[1], at)

    for number in range(4, 8):
        loads[number].wait()
    for g in range(8):
        cols = slice(g * 128, g * 128 + 128)
        even, odd = pack(exp_v[0:16, cols], exp_v[16:32, cols])
        exp_send[g * 32 : g * 32 + 16, :] = even
        exp_send[g * 32 + 16 : g * 32 + 32, :] = odd
    for k, at in x_peers:
        push(exp_send.at[rows_of(k, PIECE)], exp_recv.at[rows_of(gx, PIECE)], exp_sem.at[0], exp_sem.at[1], at)
    exp_recv[rows_of(gx, PIECE), :] = exp_send[rows_of(gx, PIECE), :]

    sum_counts()
    send_v[SUMS] = lines(sums_v)
    for k, at in x_peers:
        push(send_v.at[SUMS, rows_of(k, 32)], recv_v.at[SUMS, rows_of(gx, 32)], sums_sem.at[0], sums_sem.at[1], at)
    recv_v[SUMS, rows_of(gx, 32), :] = send_v[SUMS, rows_of(gx, 32), :]

    other = {"gy": gy + 1 - 2 * core}
    fy_half = fy_v.at[:, core]
    fy_part = recv_v.at[Y_IN, pl.ds(0, 7 * 32)]
    bytes_of(fy_part, fy_sem.at[1])
    push(fy_half, fy_half, fy_sem.at[2], fy_sem.at[3], other)
    bytes_of(fy_half, fy_sem.at[3])
    fy = fy_v[...].reshape(256, 256)
    fy_parts = split(fy)
    for half in range(2):
        arrived(Y_IN, half)
        y_mix(Y_IN, Y_OUT, half, fy_parts)
        exchange(Y_OUT, half, j, y_peers)

    fx_eighth = fx_v.at[0, pl.ds(0, N - 1), 0]
    bytes_of(fx_eighth, fx_sem.at[1])
    for step in (2, 1, 3):
        at = {"gy": lax.rem(row + step, 4) * 2 + core}
        push(fx_v.at[core, :, row], fx_v.at[core, :, row], fx_sem.at[2], fx_sem.at[3], at)
    fyt_parts[0], fyt_parts[1] = split(jnp.transpose(fy))
    for half in range(2):
        arrived(Y_OUT, half)
        turn(lambda n: recv_v[Y_OUT, pl.ds(half * HALF + n, N, stride=N), :], X_IN, half)
        exchange(X_IN, half, gx, x_peers)

    fx_half = fx_v.at[0, :, pl.ds(0, 3)]
    bytes_of(fx_half, fx_sem.at[3])
    push(fx_v.at[core], fx_v.at[core], fx_sem.at[4], fx_sem.at[5], other)
    bytes_of(fx_v.at[0], fx_sem.at[5])
    fx = jnp.concatenate([fx_v[0].reshape(ROWS, 256), fx_v[1].reshape(ROWS, 256)], axis=1)
    fx_parts[0], fx_parts[1] = split(fx)
    turned = split(jnp.transpose(fx))
    for part in range(2):
        for half in range(2):
            for k in range(N):
                x = k * 32 + half * 16
                fxt_parts[part, half, k * 16 : k * 16 + 16, :] = turned[part][x : x + 16, :]

    for half in range(2):
        arrived(X_IN, half)
    gathered = jnp.concatenate(
        [recv_v[X_IN, pl.ds(half * HALF + k * PIECE, PIECE), :] for k in range(N) for half in range(2)], axis=0
    )
    field = dot_wide((fx_parts[0], fx_parts[1]), split(gathered)) * LOG2E
    for k in range(N):
        first, second = pack(field[k * 32 : k * 32 + 16], field[k * 32 + 16 : k * 32 + 32])
        field_v[0, k * 16 : k * 16 + 16, :] = first
        field_v[1, k * 16 : k * 16 + 16, :] = second
    sums_part = recv_v.at[SUMS, pl.ds(0, ROWS - 32)]
    bytes_of(exp_recv.at[pl.ds(0, (N - 1) * 16)], exp_sem.at[1])
    bytes_of(sums_part, sums_sem.at[1])

    for begin in range(0, HALF, GROUP):
        rows = slice(begin, begin + GROUP)
        f0 = field_v[0, rows, :]
        f1 = field_v[1, rows, :]

        def mark(m, total):
            l0 = load_ref[0, m]
            l1 = load_ref[1, m]
            rate = jnp.exp2(l0 * f0 + (l1 * f1 + (off_ref[m] * LOG2E - SHIFT)))
            return total[0] + l0 * rate, total[1] + l1 * rate

        zero = jnp.zeros((GROUP, 128), F32)
        field_v[0, rows, :], field_v[1, rows, :] = lax.fori_loop(0, MARKS, mark, (zero, zero), unroll=16)

    residual = []
    for k in range(N):
        rows = slice(k * 16, k * 16 + 16)
        scale = exp_recv[rows, :] * (2.0**SHIFT)
        residual += pack(scale * field_v[0, rows, :], scale * field_v[1, rows, :])
    back = split(dot(split(recv_v[SUMS] - jnp.concatenate(residual, axis=0)), time))
    for half in range(2):
        send_v[X_OUT, pl.ds(half * HALF, HALF), :] = dot_wide((fxt_parts[0, half], fxt_parts[1, half]), back)
        exchange(X_OUT, half, gx, x_peers)
    for half in range(2):
        arrived(X_OUT, half)
        turn(lambda n: recv_v[X_OUT, pl.ds(half * HALF + n, N, stride=N), :], BY_IN, half)
        exchange(BY_IN, half, j, y_peers)
    for half in range(2):
        arrived(BY_IN, half)
        y_mix(BY_IN, BY_OUT, half, (fyt_parts[0], fyt_parts[1]))
        exchange(BY_OUT, half, j, y_peers)
    for half in range(2):
        arrived(BY_OUT, half)
        xs = slice(half * 16, half * 16 + 16)
        for g in range(8):
            cols = slice(g * 128, g * 128 + 128)
            out_ref[0, xs, cols], out_ref[1, xs, cols] = pack(
                recv_v[BY_OUT, pl.ds(half * HALF + 2 * g, N, stride=N), :],
                recv_v[BY_OUT, pl.ds(half * HALF + 2 * g + 1, N, stride=N), :],
            )

    for phase in range(6):
        for half in range(2):
            sent(phase, half)
    bytes_of(sums_part, sums_sem.at[0])
    bytes_of(exp_send.at[pl.ds(0, (N - 1) * 16)], exp_sem.at[0])
    bytes_of(fy_part, fy_sem.at[0])
    bytes_of(fy_half, fy_sem.at[2])
    bytes_of(fx_eighth, fx_sem.at[0])
    bytes_of(fx_half, fx_sem.at[2])
    bytes_of(fx_v.at[0], fx_sem.at[4])


def body(whitened, factor_x, factor_y, factor_t, mark_loadings, mark_offsets, exposure, counts):
    back = pl.pallas_call(
        kernel,
        out_shape=jax.ShapeDtypeStruct((2, 32, 1024), F32),
        in_specs=[pl.BlockSpec(memory_space=pltpu.HBM)] * 8,
        out_specs=pl.BlockSpec(memory_space=pltpu.VMEM),
        scratch_shapes=[
            pltpu.SMEM((2, MARKS), F32),
            pltpu.SMEM((MARKS,), F32),
            pltpu.VMEM((2, 32, 1024), F32),
            pltpu.VMEM((32, 1024), F32),
            pltpu.VMEM((MARKS, 32, 1024), jnp.int32),
            pltpu.VMEM((2, 32, 1024), F32),
            pltpu.VMEM((64, 64), F32),
            pltpu.VMEM((2, N, 4, 8, 256), F32),
            pltpu.VMEM((2, 512, 512), BF16),
            pltpu.VMEM((2, 2, HALF, 512), BF16),
            pltpu.VMEM((4, 2, 2, 16, 256), F32),
            pltpu.VMEM((2, 256, 256), BF16),
            pltpu.VMEM((ROWS, 128), F32),
            pltpu.VMEM((2, HALF, 128), F32),
            pltpu.VMEM((7, ROWS, 128), F32),
            pltpu.VMEM((7, ROWS, 128), F32),
            pltpu.VMEM((256, 128), F32),
            pltpu.VMEM((256, 128), F32),
            pltpu.SemaphoreType.DMA((8,)),
            pltpu.SemaphoreType.DMA((6, 2)),
            pltpu.SemaphoreType.DMA((6, 2)),
            pltpu.SemaphoreType.DMA((2,)),
            pltpu.SemaphoreType.DMA((2,)),
            pltpu.SemaphoreType.DMA((6,)),
            pltpu.SemaphoreType.DMA((4,)),
        ],
        compiler_params=pltpu.CompilerParams(
            collective_id=0, has_side_effects=True, vmem_limit_bytes=60 * 1024 * 1024
        ),
    )(mark_loadings, mark_offsets, whitened, factor_x, factor_y, factor_t, exposure, counts)
    return back - whitened


def solution(mesh):
    placed = (
        P(None, "gx", ("gy", "ta")),
        P("gx", None),
        P(("gy", "ta"), None),
        P(),
        P(),
        P(),
        P("gx", ("gy", "ta")),
        P(None, "gx", ("gy", "ta")),
    )
    return jax.shard_map(
        body, mesh=mesh, in_specs=placed, out_specs=P(None, "gx", ("gy", "ta")), check_vma=False
    )
```

```python
import math

import jax
import jax.numpy as jnp
from jax import lax
from jax.experimental import pallas as pl
from jax.experimental.pallas import tpu as pltpu
from jax.sharding import PartitionSpec as P

MESH = pl.DeviceIdType.MESH
F32 = jnp.float32
BF16 = jnp.bfloat16
LOG2E = math.log2(math.e)
N = 16
PIECE = 16
HALF = N * PIECE
ROWS = 2 * HALF
MARKS = 64
SHIFT = 8.0
GROUP = 64
Y_IN, Y_OUT, X_IN, X_OUT, BY_IN, BY_OUT, SUMS = range(7)
X_STEPS = sorted(
    [(z, x) for z in range(8) for x in range(2) if z or x], key=lambda s: -(min(s[0], 8 - s[0]) + 2 * s[1])
)
Y_STEPS = sorted(
    [(y, c, x) for y in range(4) for c in range(2) for x in range(2) if y or c or x],
    key=lambda s: -(min(s[0], 4 - s[0]) + s[2]),
)


def split(a):
    high = a.astype(BF16)
    return high, (a - high.astype(F32)).astype(BF16)


def dot(a, b, dims=((1,), (0,))):
    def one(left, right):
        return lax.dot_general(left, right, (dims, ((), ())), preferred_element_type=F32)

    return one(a[0], b[0]) + (one(a[0], b[1]) + one(a[1], b[0]))


def dot_wide(a, b):
    both = jnp.dot(a[0], jnp.concatenate([b[0], b[1]], axis=1), preferred_element_type=F32)
    return both[:, :128] + (both[:, 128:] + jnp.dot(a[1], b[0], preferred_element_type=F32))


def swap_halves(a):
    return pltpu.roll(a, 64, 1)


def kernel(
    load_hbm, off_hbm, w_hbm, fx_hbm, fy_hbm, ft_hbm, exp_hbm, counts_hbm, out_ref,
    load_ref, off_ref, rate_off, w_v, exp_v, counts_v, sums_v, ft_v,
    fx_v, fx_parts, fxt_parts, fy_v, fyt_parts,
    t_v, field_v, send_v, recv_v, exp_send, exp_recv,
    local_sem, send_sem, recv_sem, sums_sem, exp_sem, fx_sem, fy_sem,
):
    gx = lax.axis_index("gx")
    gy = lax.axis_index("gy")
    ta = lax.axis_index("ta")
    j = gy * 2 + ta
    core = lax.rem(gy, 2)
    row = gy // 2

    def x_peer(step):
        x = gx // 8
        k = (x + step[1] - 2 * x * step[1]) * 8 + lax.rem(gx + step[0], 8)
        return k, {"gx": k}

    def y_peer(step):
        y = lax.rem(gy // 2 + step[0], 4)
        a = y * 2 + (core + step[1] - 2 * core * step[1])
        b = ta + step[2] - 2 * ta * step[2]
        return a * 2 + b, {"gy": a, "ta": b}

    x_peers = [x_peer(step) for step in X_STEPS]
    y_peers = [y_peer(step) for step in Y_STEPS]

    barrier = pltpu.get_barrier_semaphore()
    for _, at in x_peers + y_peers:
        pl.semaphore_signal(barrier, inc=1, device_id=at, device_id_type=MESH)

    loads = []
    for number, (source, target) in enumerate(
        (
            (w_hbm, w_v),
            (ft_hbm, ft_v),
            (fy_hbm, fy_v.at[row, core, ta]),
            (
                fx_hbm.at[pl.ds(pl.multiple_of(row * 8, 8), 8), pl.ds(pl.multiple_of(core * 256, 256), 256)],
                fx_v.at[core, gx, row],
            ),
            (load_hbm, load_ref),
            (off_hbm, off_ref),
            (exp_hbm, exp_v),
            (counts_hbm, counts_v),
        )
    ):
        loads.append(pltpu.make_async_copy(source, target, local_sem.at[number]))
        loads[-1].start()

    def push(source, target, sends, receives, at):
        pltpu.make_async_remote_copy(
            src_ref=source, dst_ref=target, send_sem=sends, recv_sem=receives, device_id=at, device_id_type=MESH
        ).start()

    def rows_of(k, piece, base=0):
        return pl.ds(pl.multiple_of(base + k * piece, piece), piece)

    def exchange(phase, half, me, peers):
        mine = rows_of(me, PIECE, half * HALF)
        for k, at in peers:
            push(
                send_v.at[phase, rows_of(k, PIECE, half * HALF)],
                recv_v.at[phase, mine],
                send_sem.at[phase, half],
                recv_sem.at[phase, half],
                at,
            )
        recv_v[phase, mine, :] = send_v[phase, mine, :]

    def bytes_of(part, sem):
        pltpu.make_async_copy(part, part, sem).wait()

    def arrived(phase, half):
        bytes_of(recv_v.at[phase, pl.ds(0, HALF - PIECE)], recv_sem.at[phase, half])

    def sent(phase, half):
        bytes_of(send_v.at[phase, pl.ds(0, HALF - PIECE)], send_sem.at[phase, half])

    def low(rows):
        return lax.broadcasted_iota(jnp.int32, (rows, 128), 1) < 64

    def pack(first, second):
        half = low(first.shape[0])
        return jnp.where(half, first, swap_halves(second)), jnp.where(half, swap_halves(first), second)

    def lines(ref):
        found = []
        for g in range(8):
            found += pack(ref[0, :, g * 128 : g * 128 + 128], ref[1, :, g * 128 : g * 128 + 128])
        return jnp.concatenate(found, axis=0)

    def turn(load, phase, half):
        for n in range(N):
            send_v[phase, pl.ds(half * HALF + n * N, N), :] = load(n)

    def y_mix(source, target, half, matrix):
        rows = pl.ds(half * HALF, HALF)
        send_v[target, rows, :] = dot_wide(matrix, split(recv_v[source, rows, :]))

    def sum_counts():
        for xt in range(4):
            xs = slice(xt * 8, xt * 8 + 8)

            def mark(m, total):
                tile = counts_v[m, xs, :].astype(F32)
                return total[0] + load_ref[0, m] * tile, total[1] + load_ref[1, m] * tile

            zero = jnp.zeros((8, 1024), F32)
            sums_v[0, xs, :], sums_v[1, xs, :] = lax.fori_loop(0, MARKS, mark, (zero, zero), unroll=4)

    for number in range(4):
        loads[number].wait()
    nothing = jnp.zeros((64, 64), F32)
    time = split(
        jnp.concatenate(
            [jnp.concatenate([ft_v[...], nothing], axis=1), jnp.concatenate([nothing, ft_v[...]], axis=1)], axis=0
        )
    )
    t_v[...] = dot(split(lines(w_v)), time, ((1,), (1,)))
    for half in range(2):
        turn(lambda n: t_v[pl.ds(half * N + n, N, stride=32), :], Y_IN, half)

    pl.semaphore_wait(barrier, 2 * (N - 1))

    mine = fy_v.at[row, core, ta]
    for step, (_, at) in zip(Y_STEPS, y_peers):
        if step[1] == 0:
            push(mine, mine, fy_sem.at[0], fy_sem.at[1], at)
    for half in range(2):
        exchange(Y_IN, half, j, y_peers)
    for number in range(4, 8):
        loads[number].wait()
    for g in range(8):
        cols = slice(g * 128, g * 128 + 128)
        even, odd = pack(exp_v[0:16, cols], exp_v[16:32, cols])
        exp_send[g * 32 : g * 32 + 16, :] = even
        exp_send[g * 32 + 16 : g * 32 + 32, :] = odd
    sum_counts()

    for _, at in x_peers:
        push(fx_v.at[core, gx, row], fx_v.at[core, gx, row], fx_sem.at[0], fx_sem.at[1], at)
    for k, at in x_peers:
        push(exp_send.at[rows_of(k, PIECE)], exp_recv.at[rows_of(gx, PIECE)], exp_sem.at[0], exp_sem.at[1], at)
    exp_recv[rows_of(gx, PIECE), :] = exp_send[rows_of(gx, PIECE), :]

    def scale_offset(m, carry):
        rate_off[m] = off_ref[m] * LOG2E - SHIFT
        return carry

    lax.fori_loop(0, MARKS, scale_offset, 0)
    send_v[SUMS] = lines(sums_v)
    other = {"gy": gy + 1 - 2 * core}
    fy_half = fy_v.at[:, core]
    fy_part = recv_v.at[Y_IN, pl.ds(0, 7 * 32)]
    bytes_of(fy_part, fy_sem.at[1])
    push(fy_half, fy_half, fy_sem.at[2], fy_sem.at[3], other)
    bytes_of(fy_half, fy_sem.at[3])
    fy = fy_v[...].reshape(256, 256)
    fy_parts = split(fy)
    for half in range(2):
        arrived(Y_IN, half)
        y_mix(Y_IN, Y_OUT, half, fy_parts)
        exchange(Y_OUT, half, j, y_peers)
        if half == 0:
            for k, at in x_peers:
                push(send_v.at[SUMS, rows_of(k, 32)], recv_v.at[SUMS, rows_of(gx, 32)], sums_sem.at[0], sums_sem.at[1], at)
            recv_v[SUMS, rows_of(gx, 32), :] = send_v[SUMS, rows_of(gx, 32), :]

    fx_eighth = fx_v.at[0, pl.ds(0, N - 1), 0]
    bytes_of(fx_eighth, fx_sem.at[1])
    for step in (2, 1, 3):
        at = {"gy": lax.rem(row + step, 4) * 2 + core}
        push(fx_v.at[core, :, row], fx_v.at[core, :, row], fx_sem.at[2], fx_sem.at[3], at)
    fyt_parts[0], fyt_parts[1] = split(jnp.transpose(fy))
    for half in range(2):
        arrived(Y_OUT, half)
        turn(lambda n: recv_v[Y_OUT, pl.ds(half * HALF + n, N, stride=N), :], X_IN, half)
        exchange(X_IN, half, gx, x_peers)

    fx_half = fx_v.at[0, :, pl.ds(0, 3)]
    bytes_of(fx_half, fx_sem.at[3])
    push(fx_v.at[core], fx_v.at[core], fx_sem.at[4], fx_sem.at[5], other)
    bytes_of(fx_v.at[0], fx_sem.at[5])
    fx = jnp.concatenate([fx_v[0].reshape(ROWS, 256), fx_v[1].reshape(ROWS, 256)], axis=1)
    fx_parts[0], fx_parts[1] = split(fx)
    turned = split(jnp.transpose(fx))
    for part in range(2):
        for half in range(2):
            for k in range(N):
                x = k * 32 + half * 16
                fxt_parts[part, half, k * 16 : k * 16 + 16, :] = turned[part][x : x + 16, :]

    for half in range(2):
        arrived(X_IN, half)
    gathered = jnp.concatenate(
        [recv_v[X_IN, pl.ds(half * HALF + k * PIECE, PIECE), :] for k in range(N) for half in range(2)], axis=0
    )
    field = dot_wide((fx_parts[0], fx_parts[1]), split(gathered)) * LOG2E
    for k in range(N):
        first, second = pack(field[k * 32 : k * 32 + 16], field[k * 32 + 16 : k * 32 + 32])
        field_v[0, k * 16 : k * 16 + 16, :] = first
        field_v[1, k * 16 : k * 16 + 16, :] = second
    sums_part = recv_v.at[SUMS, pl.ds(0, ROWS - 32)]
    bytes_of(exp_recv.at[pl.ds(0, (N - 1) * 16)], exp_sem.at[1])
    bytes_of(sums_part, sums_sem.at[1])

    for begin in range(0, HALF, GROUP):
        rows = slice(begin, begin + GROUP)
        f0 = field_v[0, rows, :]
        f1 = field_v[1, rows, :]

        def mark(m, total):
            l0 = load_ref[0, m]
            l1 = load_ref[1, m]
            rate = jnp.exp2(l0 * f0 + (l1 * f1 + rate_off[m]))
            return total[0] + l0 * rate, total[1] + l1 * rate

        zero = jnp.zeros((GROUP, 128), F32)
        field_v[0, rows, :], field_v[1, rows, :] = lax.fori_loop(0, MARKS, mark, (zero, zero), unroll=16)

    residual = []
    for k in range(N):
        rows = slice(k * 16, k * 16 + 16)
        scale = exp_recv[rows, :] * (2.0**SHIFT)
        residual += pack(scale * field_v[0, rows, :], scale * field_v[1, rows, :])
    back = split(dot(split(recv_v[SUMS] - jnp.concatenate(residual, axis=0)), time))
    for half in range(2):
        send_v[X_OUT, pl.ds(half * HALF, HALF), :] = dot_wide((fxt_parts[0, half], fxt_parts[1, half]), back)
        exchange(X_OUT, half, gx, x_peers)
    for half in range(2):
        arrived(X_OUT, half)
        turn(lambda n: recv_v[X_OUT, pl.ds(half * HALF + n, N, stride=N), :], BY_IN, half)
        exchange(BY_IN, half, j, y_peers)
    for half in range(2):
        arrived(BY_IN, half)
        y_mix(BY_IN, BY_OUT, half, (fyt_parts[0], fyt_parts[1]))
        exchange(BY_OUT, half, j, y_peers)
    for half in range(2):
        arrived(BY_OUT, half)
        xs = slice(half * 16, half * 16 + 16)
        for g in range(8):
            cols = slice(g * 128, g * 128 + 128)
            out_ref[0, xs, cols], out_ref[1, xs, cols] = pack(
                recv_v[BY_OUT, pl.ds(half * HALF + 2 * g, N, stride=N), :],
                recv_v[BY_OUT, pl.ds(half * HALF + 2 * g + 1, N, stride=N), :],
            )

    for phase in range(6):
        for half in range(2):
            sent(phase, half)
    bytes_of(sums_part, sums_sem.at[0])
    bytes_of(exp_send.at[pl.ds(0, (N - 1) * 16)], exp_sem.at[0])
    bytes_of(fy_part, fy_sem.at[0])
    bytes_of(fy_half, fy_sem.at[2])
    bytes_of(fx_eighth, fx_sem.at[0])
    bytes_of(fx_half, fx_sem.at[2])
    bytes_of(fx_v.at[0], fx_sem.at[4])


def body(whitened, factor_x, factor_y, factor_t, mark_loadings, mark_offsets, exposure, counts):
    back = pl.pallas_call(
        kernel,
        out_shape=jax.ShapeDtypeStruct((2, 32, 1024), F32),
        in_specs=[pl.BlockSpec(memory_space=pltpu.HBM)] * 8,
        out_specs=pl.BlockSpec(memory_space=pltpu.VMEM),
        scratch_shapes=[
            pltpu.SMEM((2, MARKS), F32),
            pltpu.SMEM((MARKS,), F32),
            pltpu.SMEM((MARKS,), F32),
            pltpu.VMEM((2, 32, 1024), F32),
            pltpu.VMEM((32, 1024), F32),
            pltpu.VMEM((MARKS, 32, 1024), jnp.int32),
            pltpu.VMEM((2, 32, 1024), F32),
            pltpu.VMEM((64, 64), F32),
            pltpu.VMEM((2, N, 4, 8, 256), F32),
            pltpu.VMEM((2, 512, 512), BF16),
            pltpu.VMEM((2, 2, HALF, 512), BF16),
            pltpu.VMEM((4, 2, 2, 16, 256), F32),
            pltpu.VMEM((2, 256, 256), BF16),
            pltpu.VMEM((ROWS, 128), F32),
            pltpu.VMEM((2, HALF, 128), F32),
            pltpu.VMEM((7, ROWS, 128), F32),
            pltpu.VMEM((7, ROWS, 128), F32),
            pltpu.VMEM((256, 128), F32),
            pltpu.VMEM((256, 128), F32),
            pltpu.SemaphoreType.DMA((8,)),
            pltpu.SemaphoreType.DMA((6, 2)),
            pltpu.SemaphoreType.DMA((6, 2)),
            pltpu.SemaphoreType.DMA((2,)),
            pltpu.SemaphoreType.DMA((2,)),
            pltpu.SemaphoreType.DMA((6,)),
            pltpu.SemaphoreType.DMA((4,)),
        ],
        compiler_params=pltpu.CompilerParams(
            collective_id=0, has_side_effects=True, vmem_limit_bytes=60 * 1024 * 1024
        ),
    )(mark_loadings, mark_offsets, whitened, factor_x, factor_y, factor_t, exposure, counts)
    return back - whitened


def solution(mesh):
    placed = (
        P(None, "gx", ("gy", "ta")),
        P("gx", None),
        P(("gy", "ta"), None),
        P(),
        P(),
        P(),
        P("gx", ("gy", "ta")),
        P(None, "gx", ("gy", "ta")),
    )
    return jax.shard_map(
        body, mesh=mesh, in_specs=placed, out_specs=P(None, "gx", ("gy", "ta")), check_vma=False
    )
```

```python
import math

import jax
import jax.numpy as jnp
from jax import lax
from jax.experimental import pallas as pl
from jax.experimental.pallas import tpu as pltpu
from jax.sharding import PartitionSpec as P

MESH = pl.DeviceIdType.MESH
F32 = jnp.float32
BF16 = jnp.bfloat16
LOG2E = math.log2(math.e)
N = 16
PIECE = 16
HALF = N * PIECE
ROWS = 2 * HALF
MARKS = 64
SHIFT = 8.0
GROUP = 64
Y_IN, Y_OUT, X_IN, X_OUT, BY_IN, BY_OUT, SUMS = range(7)
X_STEPS = sorted(
    [(z, x) for z in range(8) for x in range(2) if z or x], key=lambda s: -(min(s[0], 8 - s[0]) + 2 * s[1])
)
Y_STEPS = sorted(
    [(y, c, x) for y in range(4) for c in range(2) for x in range(2) if y or c or x],
    key=lambda s: -(min(s[0], 4 - s[0]) + s[2]),
)


def split(a):
    high = a.astype(BF16)
    return high, (a - high.astype(F32)).astype(BF16)


def dot(a, b, dims=((1,), (0,))):
    def one(left, right):
        return lax.dot_general(left, right, (dims, ((), ())), preferred_element_type=F32)

    return one(a[0], b[0]) + (one(a[0], b[1]) + one(a[1], b[0]))


def dot_wide(a, b):
    both = jnp.dot(a[0], jnp.concatenate([b[0], b[1]], axis=1), preferred_element_type=F32)
    return both[:, :128] + (both[:, 128:] + jnp.dot(a[1], b[0], preferred_element_type=F32))


def swap_halves(a):
    return pltpu.roll(a, 64, 1)


def kernel(
    load_hbm, off_hbm, w_hbm, fx_hbm, fy_hbm, ft_hbm, exp_hbm, counts_hbm, out_ref,
    load_ref, off_ref, rate_off, w_v, exp_v, counts_v, sums_v, ft_v,
    fx_v, fx_parts, fxt_parts, fy_v, fyt_parts,
    t_v, field_v, send_v, recv_v, exp_send, exp_recv,
    local_sem, send_sem, recv_sem, sums_sem, exp_sem, fx_sem, fy_sem,
):
    gx = lax.axis_index("gx")
    gy = lax.axis_index("gy")
    ta = lax.axis_index("ta")
    j = gy * 2 + ta
    core = lax.rem(gy, 2)
    row = gy // 2

    def x_peer(step):
        x = gx // 8
        k = (x + step[1] - 2 * x * step[1]) * 8 + lax.rem(gx + step[0], 8)
        return k, {"gx": k}

    def y_peer(step):
        y = lax.rem(gy // 2 + step[0], 4)
        a = y * 2 + (core + step[1] - 2 * core * step[1])
        b = ta + step[2] - 2 * ta * step[2]
        return a * 2 + b, {"gy": a, "ta": b}

    x_peers = [x_peer(step) for step in X_STEPS]
    y_peers = [y_peer(step) for step in Y_STEPS]

    barrier = pltpu.get_barrier_semaphore()
    for _, at in x_peers + y_peers:
        pl.semaphore_signal(barrier, inc=1, device_id=at, device_id_type=MESH)

    loads = []
    for number, (source, target) in enumerate(
        (
            (w_hbm, w_v),
            (ft_hbm, ft_v),
            (fy_hbm, fy_v.at[row, core, ta]),
            (
                fx_hbm.at[pl.ds(pl.multiple_of(row * 8, 8), 8), pl.ds(pl.multiple_of(core * 256, 256), 256)],
                fx_v.at[core, gx, row],
            ),
            (load_hbm, load_ref),
            (off_hbm, off_ref),
            (exp_hbm, exp_v),
            (counts_hbm, counts_v),
        )
    ):
        loads.append(pltpu.make_async_copy(source, target, local_sem.at[number]))
        loads[-1].start()

    def push(source, target, sends, receives, at):
        pltpu.make_async_remote_copy(
            src_ref=source, dst_ref=target, send_sem=sends, recv_sem=receives, device_id=at, device_id_type=MESH
        ).start()

    def rows_of(k, piece, base=0):
        return pl.ds(pl.multiple_of(base + k * piece, piece), piece)

    def exchange(phase, half, me, peers):
        mine = rows_of(me, PIECE, half * HALF)
        for k, at in peers:
            push(
                send_v.at[phase, rows_of(k, PIECE, half * HALF)],
                recv_v.at[phase, mine],
                send_sem.at[phase, half],
                recv_sem.at[phase, half],
                at,
            )
        recv_v[phase, mine, :] = send_v[phase, mine, :]

    def bytes_of(part, sem):
        pltpu.make_async_copy(part, part, sem).wait()

    def arrived(phase, half):
        bytes_of(recv_v.at[phase, pl.ds(0, HALF - PIECE)], recv_sem.at[phase, half])

    def sent(phase, half):
        bytes_of(send_v.at[phase, pl.ds(0, HALF - PIECE)], send_sem.at[phase, half])

    def low(rows):
        return lax.broadcasted_iota(jnp.int32, (rows, 128), 1) < 64

    def pack(first, second):
        half = low(first.shape[0])
        return jnp.where(half, first, swap_halves(second)), jnp.where(half, swap_halves(first), second)

    def lines(ref):
        found = []
        for g in range(8):
            found += pack(ref[0, :, g * 128 : g * 128 + 128], ref[1, :, g * 128 : g * 128 + 128])
        return jnp.concatenate(found, axis=0)

    def turn(load, phase, half):
        for n in range(N):
            send_v[phase, pl.ds(half * HALF + n * N, N), :] = load(n)

    def y_mix(source, target, half, matrix):
        rows = pl.ds(half * HALF, HALF)
        send_v[target, rows, :] = dot_wide(matrix, split(recv_v[source, rows, :]))

    def sum_counts():
        for xt in range(4):
            xs = slice(xt * 8, xt * 8 + 8)

            def mark(m, total):
                tile = counts_v[m, xs, :].astype(F32)
                return total[0] + load_ref[0, m] * tile, total[1] + load_ref[1, m] * tile

            zero = jnp.zeros((8, 1024), F32)
            sums_v[0, xs, :], sums_v[1, xs, :] = lax.fori_loop(0, MARKS, mark, (zero, zero), unroll=4)

    for number in range(4):
        loads[number].wait()
    nothing = jnp.zeros((64, 64), F32)
    time = split(
        jnp.concatenate(
            [jnp.concatenate([ft_v[...], nothing], axis=1), jnp.concatenate([nothing, ft_v[...]], axis=1)], axis=0
        )
    )
    t_v[...] = dot(split(lines(w_v)), time, ((1,), (1,)))
    for half in range(2):
        turn(lambda n: t_v[pl.ds(half * N + n, N, stride=32), :], Y_IN, half)

    pl.semaphore_wait(barrier, 2 * (N - 1))

    mine = fy_v.at[row, core, ta]
    for step, (_, at) in zip(Y_STEPS, y_peers):
        if step[1] == 0:
            push(mine, mine, fy_sem.at[0], fy_sem.at[1], at)
    for half in range(2):
        exchange(Y_IN, half, j, y_peers)
    for number in range(4, 8):
        loads[number].wait()
    for g in range(8):
        cols = slice(g * 128, g * 128 + 128)
        even, odd = pack(exp_v[0:16, cols], exp_v[16:32, cols])
        exp_send[g * 32 : g * 32 + 16, :] = even
        exp_send[g * 32 + 16 : g * 32 + 32, :] = odd
    sum_counts()

    for _, at in x_peers:
        push(fx_v.at[core, gx, row], fx_v.at[core, gx, row], fx_sem.at[0], fx_sem.at[1], at)
    for k, at in x_peers:
        push(exp_send.at[rows_of(k, PIECE)], exp_recv.at[rows_of(gx, PIECE)], exp_sem.at[0], exp_sem.at[1], at)
    exp_recv[rows_of(gx, PIECE), :] = exp_send[rows_of(gx, PIECE), :]

    def scale_offset(m, carry):
        rate_off[m] = off_ref[m] * LOG2E - SHIFT
        return carry

    lax.fori_loop(0, MARKS, scale_offset, 0)
    send_v[SUMS] = lines(sums_v)
    other = {"gy": gy + 1 - 2 * core}
    fy_half = fy_v.at[:, core]
    fy_part = recv_v.at[Y_IN, pl.ds(0, 7 * 32)]
    bytes_of(fy_part, fy_sem.at[1])
    push(fy_half, fy_half, fy_sem.at[2], fy_sem.at[3], other)
    bytes_of(fy_half, fy_sem.at[3])
    fy = fy_v[...].reshape(256, 256)
    fy_parts = split(fy)
    for half in range(2):
        arrived(Y_IN, half)
        y_mix(Y_IN, Y_OUT, half, fy_parts)
        exchange(Y_OUT, half, j, y_peers)
        if half == 0:
            for k, at in x_peers:
                push(send_v.at[SUMS, rows_of(k, 32)], recv_v.at[SUMS, rows_of(gx, 32)], sums_sem.at[0], sums_sem.at[1], at)
            recv_v[SUMS, rows_of(gx, 32), :] = send_v[SUMS, rows_of(gx, 32), :]

    fx_eighth = fx_v.at[0, pl.ds(0, N - 1), 0]
    bytes_of(fx_eighth, fx_sem.at[1])
    for step in (2, 1, 3):
        at = {"gy": lax.rem(row + step, 4) * 2 + core}
        push(fx_v.at[core, :, row], fx_v.at[core, :, row], fx_sem.at[2], fx_sem.at[3], at)
    fyt_parts[0], fyt_parts[1] = split(jnp.transpose(fy))
    for half in range(2):
        arrived(Y_OUT, half)
        turn(lambda n: recv_v[Y_OUT, pl.ds(half * HALF + n, N, stride=N), :], X_IN, half)
        exchange(X_IN, half, gx, x_peers)

    fx_half = fx_v.at[0, :, pl.ds(0, 3)]
    bytes_of(fx_half, fx_sem.at[3])
    push(fx_v.at[core], fx_v.at[core], fx_sem.at[4], fx_sem.at[5], other)
    bytes_of(fx_v.at[0], fx_sem.at[5])
    fx = jnp.concatenate([fx_v[0].reshape(ROWS, 256), fx_v[1].reshape(ROWS, 256)], axis=1)
    fx_parts[0], fx_parts[1] = split(fx)
    turned = split(jnp.transpose(fx))
    for part in range(2):
        for half in range(2):
            for k in range(N):
                x = k * 32 + half * 16
                fxt_parts[part, half, k * 16 : k * 16 + 16, :] = turned[part][x : x + 16, :]

    for half in range(2):
        arrived(X_IN, half)
    gathered = jnp.concatenate(
        [recv_v[X_IN, pl.ds(half * HALF + k * PIECE, PIECE), :] for k in range(N) for half in range(2)], axis=0
    )
    field = dot_wide((fx_parts[0], fx_parts[1]), split(gathered)) * LOG2E
    for k in range(N):
        first, second = pack(field[k * 32 : k * 32 + 16], field[k * 32 + 16 : k * 32 + 32])
        field_v[0, k * 16 : k * 16 + 16, :] = first
        field_v[1, k * 16 : k * 16 + 16, :] = second
    sums_part = recv_v.at[SUMS, pl.ds(0, ROWS - 32)]
    bytes_of(exp_recv.at[pl.ds(0, (N - 1) * 16)], exp_sem.at[1])
    bytes_of(sums_part, sums_sem.at[1])

    for begin in range(0, HALF, GROUP):
        rows = slice(begin, begin + GROUP)
        f0 = field_v[0, rows, :]
        f1 = field_v[1, rows, :]

        def mark(m, total):
            l0 = load_ref[0, m]
            l1 = load_ref[1, m]
            rate = jnp.exp2(l0 * f0 + (l1 * f1 + rate_off[m]))
            return total[0] + l0 * rate, total[1] + l1 * rate

        zero = jnp.zeros((GROUP, 128), F32)
        field_v[0, rows, :], field_v[1, rows, :] = lax.fori_loop(0, MARKS, mark, (zero, zero), unroll=16)

    residual = []
    for k in range(N):
        rows = slice(k * 16, k * 16 + 16)
        scale = exp_recv[rows, :] * (2.0**SHIFT)
        residual += pack(scale * field_v[0, rows, :], scale * field_v[1, rows, :])
    back = split(recv_v[SUMS] - jnp.concatenate(residual, axis=0))
    for half in range(2):
        send_v[X_OUT, pl.ds(half * HALF, HALF), :] = dot_wide((fxt_parts[0, half], fxt_parts[1, half]), back)
        exchange(X_OUT, half, gx, x_peers)
    for half in range(2):
        arrived(X_OUT, half)
        turn(lambda n: recv_v[X_OUT, pl.ds(half * HALF + n, N, stride=N), :], BY_IN, half)
        exchange(BY_IN, half, j, y_peers)
    for half in range(2):
        arrived(BY_IN, half)
        y_mix(BY_IN, BY_OUT, half, (fyt_parts[0], fyt_parts[1]))
        exchange(BY_OUT, half, j, y_peers)
    for half in range(2):
        arrived(BY_OUT, half)
        xs = slice(half * 16, half * 16 + 16)
        rows = pl.ds(half * HALF, HALF)
        t_v[rows, :] = dot(split(recv_v[BY_OUT, rows, :]), time)
        for g in range(8):
            cols = slice(g * 128, g * 128 + 128)
            out_ref[0, xs, cols], out_ref[1, xs, cols] = pack(
                t_v[pl.ds(half * HALF + 2 * g, N, stride=N), :],
                t_v[pl.ds(half * HALF + 2 * g + 1, N, stride=N), :],
            )

    for phase in range(6):
        for half in range(2):
            sent(phase, half)
    bytes_of(sums_part, sums_sem.at[0])
    bytes_of(exp_send.at[pl.ds(0, (N - 1) * 16)], exp_sem.at[0])
    bytes_of(fy_part, fy_sem.at[0])
    bytes_of(fy_half, fy_sem.at[2])
    bytes_of(fx_eighth, fx_sem.at[0])
    bytes_of(fx_half, fx_sem.at[2])
    bytes_of(fx_v.at[0], fx_sem.at[4])


def body(whitened, factor_x, factor_y, factor_t, mark_loadings, mark_offsets, exposure, counts):
    back = pl.pallas_call(
        kernel,
        out_shape=jax.ShapeDtypeStruct((2, 32, 1024), F32),
        in_specs=[pl.BlockSpec(memory_space=pltpu.HBM)] * 8,
        out_specs=pl.BlockSpec(memory_space=pltpu.VMEM),
        scratch_shapes=[
            pltpu.SMEM((2, MARKS), F32),
            pltpu.SMEM((MARKS,), F32),
            pltpu.SMEM((MARKS,), F32),
            pltpu.VMEM((2, 32, 1024), F32),
            pltpu.VMEM((32, 1024), F32),
            pltpu.VMEM((MARKS, 32, 1024), jnp.int32),
            pltpu.VMEM((2, 32, 1024), F32),
            pltpu.VMEM((64, 64), F32),
            pltpu.VMEM((2, N, 4, 8, 256), F32),
            pltpu.VMEM((2, 512, 512), BF16),
            pltpu.VMEM((2, 2, HALF, 512), BF16),
            pltpu.VMEM((4, 2, 2, 16, 256), F32),
            pltpu.VMEM((2, 256, 256), BF16),
            pltpu.VMEM((ROWS, 128), F32),
            pltpu.VMEM((2, HALF, 128), F32),
            pltpu.VMEM((7, ROWS, 128), F32),
            pltpu.VMEM((7, ROWS, 128), F32),
            pltpu.VMEM((256, 128), F32),
            pltpu.VMEM((256, 128), F32),
            pltpu.SemaphoreType.DMA((8,)),
            pltpu.SemaphoreType.DMA((6, 2)),
            pltpu.SemaphoreType.DMA((6, 2)),
            pltpu.SemaphoreType.DMA((2,)),
            pltpu.SemaphoreType.DMA((2,)),
            pltpu.SemaphoreType.DMA((6,)),
            pltpu.SemaphoreType.DMA((4,)),
        ],
        compiler_params=pltpu.CompilerParams(
            collective_id=0, has_side_effects=True, vmem_limit_bytes=60 * 1024 * 1024
        ),
    )(mark_loadings, mark_offsets, whitened, factor_x, factor_y, factor_t, exposure, counts)
    return back - whitened


def solution(mesh):
    placed = (
        P(None, "gx", ("gy", "ta")),
        P("gx", None),
        P(("gy", "ta"), None),
        P(),
        P(),
        P(),
        P("gx", ("gy", "ta")),
        P(None, "gx", ("gy", "ta")),
    )
    return jax.shard_map(
        body, mesh=mesh, in_specs=placed, out_specs=P(None, "gx", ("gy", "ta")), check_vma=False
    )
```

```python
import math

import jax
import jax.numpy as jnp
from jax import lax
from jax.experimental import pallas as pl
from jax.experimental.pallas import tpu as pltpu
from jax.sharding import PartitionSpec as P

MESH = pl.DeviceIdType.MESH
F32 = jnp.float32
BF16 = jnp.bfloat16
LOG2E = math.log2(math.e)
N = 16
PIECE = 16
HALF = N * PIECE
ROWS = 2 * HALF
MARKS = 64
SHIFT = 8.0
GROUP = 64
Y_IN, Y_OUT, X_IN, X_OUT, BY_IN, BY_OUT, SUMS = range(7)
X_STEPS = sorted(
    [(z, x) for z in range(8) for x in range(2) if z or x], key=lambda s: -(min(s[0], 8 - s[0]) + 2 * s[1])
)
Y_STEPS = sorted(
    [(y, c, x) for y in range(4) for c in range(2) for x in range(2) if y or c or x],
    key=lambda s: -(min(s[0], 4 - s[0]) + s[2]),
)


def split(a):
    high = a.astype(BF16)
    return high, (a - high.astype(F32)).astype(BF16)


def dot(a, b, dims=((1,), (0,))):
    def one(left, right):
        return lax.dot_general(left, right, (dims, ((), ())), preferred_element_type=F32)

    return one(a[0], b[0]) + (one(a[0], b[1]) + one(a[1], b[0]))


def dot_wide(a, b):
    both = jnp.dot(a[0], jnp.concatenate([b[0], b[1]], axis=1), preferred_element_type=F32)
    return both[:, :128] + (both[:, 128:] + jnp.dot(a[1], b[0], preferred_element_type=F32))


def swap_halves(a):
    return pltpu.roll(a, 64, 1)


def kernel(
    load_hbm, off_hbm, w_hbm, fx_hbm, fy_hbm, ft_hbm, exp_hbm, counts_hbm, out_ref,
    load_ref, off_ref, rate_off, w_v, exp_v, counts_v, sums_v, ft_v,
    fx_v, fx_parts, fxt_parts, fy_v, fyt_parts,
    t_v, field_v, send_v, recv_v, exp_send, exp_recv,
    local_sem, send_sem, recv_sem, sums_sem, exp_sem, fx_sem, fy_sem,
):
    gx = lax.axis_index("gx")
    gy = lax.axis_index("gy")
    ta = lax.axis_index("ta")
    j = gy * 2 + ta
    core = lax.rem(gy, 2)
    row = gy // 2

    def x_peer(step):
        x = gx // 8
        k = (x + step[1] - 2 * x * step[1]) * 8 + lax.rem(gx + step[0], 8)
        return k, {"gx": k}

    def y_peer(step):
        y = lax.rem(gy // 2 + step[0], 4)
        a = y * 2 + (core + step[1] - 2 * core * step[1])
        b = ta + step[2] - 2 * ta * step[2]
        return a * 2 + b, {"gy": a, "ta": b}

    x_peers = [x_peer(step) for step in X_STEPS]
    y_peers = [y_peer(step) for step in Y_STEPS]

    barrier = pltpu.get_barrier_semaphore()
    for _, at in x_peers + y_peers:
        pl.semaphore_signal(barrier, inc=1, device_id=at, device_id_type=MESH)

    loads = []
    for number, (source, target) in enumerate(
        (
            (w_hbm, w_v),
            (ft_hbm, ft_v),
            (fy_hbm, fy_v.at[row, core, ta]),
            (
                fx_hbm.at[pl.ds(pl.multiple_of(row * 8, 8), 8), pl.ds(pl.multiple_of(core * 256, 256), 256)],
                fx_v.at[core, gx, row],
            ),
            (load_hbm, load_ref),
            (off_hbm, off_ref),
            (exp_hbm, exp_v),
            (counts_hbm, counts_v),
        )
    ):
        loads.append(pltpu.make_async_copy(source, target, local_sem.at[number]))
        loads[-1].start()

    def push(source, target, sends, receives, at):
        pltpu.make_async_remote_copy(
            src_ref=source, dst_ref=target, send_sem=sends, recv_sem=receives, device_id=at, device_id_type=MESH
        ).start()

    def rows_of(k, piece, base=0):
        return pl.ds(pl.multiple_of(base + k * piece, piece), piece)

    def exchange(phase, half, me, peers):
        mine = rows_of(me, PIECE, half * HALF)
        for k, at in peers:
            push(
                send_v.at[phase, rows_of(k, PIECE, half * HALF)],
                recv_v.at[phase, mine],
                send_sem.at[phase, half],
                recv_sem.at[phase, half],
                at,
            )
        recv_v[phase, mine, :] = send_v[phase, mine, :]

    def bytes_of(part, sem):
        pltpu.make_async_copy(part, part, sem).wait()

    def arrived(phase, half):
        bytes_of(recv_v.at[phase, pl.ds(0, HALF - PIECE)], recv_sem.at[phase, half])

    def sent(phase, half):
        bytes_of(send_v.at[phase, pl.ds(0, HALF - PIECE)], send_sem.at[phase, half])

    def low(rows):
        return lax.broadcasted_iota(jnp.int32, (rows, 128), 1) < 64

    def pack(first, second):
        half = low(first.shape[0])
        return jnp.where(half, first, swap_halves(second)), jnp.where(half, swap_halves(first), second)

    def lines(ref):
        found = []
        for g in range(8):
            found += pack(ref[0, :, g * 128 : g * 128 + 128], ref[1, :, g * 128 : g * 128 + 128])
        return jnp.concatenate(found, axis=0)

    def turn(load, phase, half):
        for n in range(N):
            send_v[phase, pl.ds(half * HALF + n * N, N), :] = load(n)

    def y_mix(source, target, half, matrix):
        rows = pl.ds(half * HALF, HALF)
        send_v[target, rows, :] = dot_wide(matrix, split(recv_v[source, rows, :]))

    def sum_counts():
        for xt in range(4):
            xs = slice(xt * 8, xt * 8 + 8)

            def mark(m, total):
                tile = counts_v[m, xs, :].astype(F32)
                return total[0] + load_ref[0, m] * tile, total[1] + load_ref[1, m] * tile

            zero = jnp.zeros((8, 1024), F32)
            sums_v[0, xs, :], sums_v[1, xs, :] = lax.fori_loop(0, MARKS, mark, (zero, zero), unroll=4)

    for number in range(4):
        loads[number].wait()
    nothing = jnp.zeros((64, 64), F32)
    time = split(
        jnp.concatenate(
            [jnp.concatenate([ft_v[...], nothing], axis=1), jnp.concatenate([nothing, ft_v[...]], axis=1)], axis=0
        )
    )
    t_v[...] = dot(split(lines(w_v)), time, ((1,), (1,)))
    for half in range(2):
        turn(lambda n: t_v[pl.ds(half * N + n, N, stride=32), :], Y_IN, half)

    pl.semaphore_wait(barrier, 2 * (N - 1))

    mine = fy_v.at[row, core, ta]
    for step, (_, at) in zip(Y_STEPS, y_peers):
        if step[1] == 0:
            push(mine, mine, fy_sem.at[0], fy_sem.at[1], at)
    for half in range(2):
        exchange(Y_IN, half, j, y_peers)
    for number in range(4, 8):
        loads[number].wait()
    for g in range(8):
        cols = slice(g * 128, g * 128 + 128)
        even, odd = pack(exp_v[0:16, cols], exp_v[16:32, cols])
        exp_send[g * 32 : g * 32 + 16, :] = even
        exp_send[g * 32 + 16 : g * 32 + 32, :] = odd
    sum_counts()

    for _, at in x_peers[::-1]:
        push(fx_v.at[core, gx, row], fx_v.at[core, gx, row], fx_sem.at[0], fx_sem.at[1], at)
    for k, at in x_peers[::-1]:
        push(exp_send.at[rows_of(k, PIECE)], exp_recv.at[rows_of(gx, PIECE)], exp_sem.at[0], exp_sem.at[1], at)
    exp_recv[rows_of(gx, PIECE), :] = exp_send[rows_of(gx, PIECE), :]

    def scale_offset(m, carry):
        rate_off[m] = off_ref[m] * LOG2E - SHIFT
        return carry

    lax.fori_loop(0, MARKS, scale_offset, 0)
    send_v[SUMS] = lines(sums_v)
    other = {"gy": gy + 1 - 2 * core}
    fy_half = fy_v.at[:, core]
    fy_part = recv_v.at[Y_IN, pl.ds(0, 7 * 32)]
    bytes_of(fy_part, fy_sem.at[1])
    push(fy_half, fy_half, fy_sem.at[2], fy_sem.at[3], other)
    bytes_of(fy_half, fy_sem.at[3])
    fy = fy_v[...].reshape(256, 256)
    fy_parts = split(fy)
    for half in range(2):
        arrived(Y_IN, half)
        y_mix(Y_IN, Y_OUT, half, fy_parts)
        exchange(Y_OUT, half, j, y_peers)
        if half == 0:
            for k, at in x_peers[::-1]:
                push(send_v.at[SUMS, rows_of(k, 32)], recv_v.at[SUMS, rows_of(gx, 32)], sums_sem.at[0], sums_sem.at[1], at)
            recv_v[SUMS, rows_of(gx, 32), :] = send_v[SUMS, rows_of(gx, 32), :]

    fx_eighth = fx_v.at[0, pl.ds(0, N - 1), 0]
    bytes_of(fx_eighth, fx_sem.at[1])
    for step in (2, 1, 3):
        at = {"gy": lax.rem(row + step, 4) * 2 + core}
        push(fx_v.at[core, :, row], fx_v.at[core, :, row], fx_sem.at[2], fx_sem.at[3], at)
    fyt_parts[0], fyt_parts[1] = split(jnp.transpose(fy))
    for half in range(2):
        arrived(Y_OUT, half)
        turn(lambda n: recv_v[Y_OUT, pl.ds(half * HALF + n, N, stride=N), :], X_IN, half)
        exchange(X_IN, half, gx, x_peers)

    fx_half = fx_v.at[0, :, pl.ds(0, 3)]
    bytes_of(fx_half, fx_sem.at[3])
    push(fx_v.at[core], fx_v.at[core], fx_sem.at[4], fx_sem.at[5], other)
    bytes_of(fx_v.at[0], fx_sem.at[5])
    fx = jnp.concatenate([fx_v[0].reshape(ROWS, 256), fx_v[1].reshape(ROWS, 256)], axis=1)
    fx_parts[0], fx_parts[1] = split(fx)
    turned = split(jnp.transpose(fx))
    for part in range(2):
        for half in range(2):
            for k in range(N):
                x = k * 32 + half * 16
                fxt_parts[part, half, k * 16 : k * 16 + 16, :] = turned[part][x : x + 16, :]

    for half in range(2):
        arrived(X_IN, half)
    gathered = jnp.concatenate(
        [recv_v[X_IN, pl.ds(half * HALF + k * PIECE, PIECE), :] for k in range(N) for half in range(2)], axis=0
    )
    field = dot_wide((fx_parts[0], fx_parts[1]), split(gathered)) * LOG2E
    for k in range(N):
        first, second = pack(field[k * 32 : k * 32 + 16], field[k * 32 + 16 : k * 32 + 32])
        field_v[0, k * 16 : k * 16 + 16, :] = first
        field_v[1, k * 16 : k * 16 + 16, :] = second
    sums_part = recv_v.at[SUMS, pl.ds(0, ROWS - 32)]
    bytes_of(exp_recv.at[pl.ds(0, (N - 1) * 16)], exp_sem.at[1])
    bytes_of(sums_part, sums_sem.at[1])

    for begin in range(0, HALF, GROUP):
        rows = slice(begin, begin + GROUP)
        f0 = field_v[0, rows, :]
        f1 = field_v[1, rows, :]

        def mark(m, total):
            l0 = load_ref[0, m]
            l1 = load_ref[1, m]
            rate = jnp.exp2(l0 * f0 + (l1 * f1 + rate_off[m]))
            return total[0] + l0 * rate, total[1] + l1 * rate

        zero = jnp.zeros((GROUP, 128), F32)
        field_v[0, rows, :], field_v[1, rows, :] = lax.fori_loop(0, MARKS, mark, (zero, zero), unroll=16)

    residual = []
    for k in range(N):
        rows = slice(k * 16, k * 16 + 16)
        scale = exp_recv[rows, :] * (2.0**SHIFT)
        residual += pack(scale * field_v[0, rows, :], scale * field_v[1, rows, :])
    back = split(recv_v[SUMS] - jnp.concatenate(residual, axis=0))
    for half in range(2):
        send_v[X_OUT, pl.ds(half * HALF, HALF), :] = dot_wide((fxt_parts[0, half], fxt_parts[1, half]), back)
        exchange(X_OUT, half, gx, x_peers)
    for half in range(2):
        arrived(X_OUT, half)
        turn(lambda n: recv_v[X_OUT, pl.ds(half * HALF + n, N, stride=N), :], BY_IN, half)
        exchange(BY_IN, half, j, y_peers)
    for half in range(2):
        arrived(BY_IN, half)
        y_mix(BY_IN, BY_OUT, half, (fyt_parts[0], fyt_parts[1]))
        exchange(BY_OUT, half, j, y_peers)
    for half in range(2):
        arrived(BY_OUT, half)
        xs = slice(half * 16, half * 16 + 16)
        rows = pl.ds(half * HALF, HALF)
        t_v[rows, :] = dot(split(recv_v[BY_OUT, rows, :]), time)
        for g in range(8):
            cols = slice(g * 128, g * 128 + 128)
            out_ref[0, xs, cols], out_ref[1, xs, cols] = pack(
                t_v[pl.ds(half * HALF + 2 * g, N, stride=N), :],
                t_v[pl.ds(half * HALF + 2 * g + 1, N, stride=N), :],
            )

    for phase in range(6):
        for half in range(2):
            sent(phase, half)
    bytes_of(sums_part, sums_sem.at[0])
    bytes_of(exp_send.at[pl.ds(0, (N - 1) * 16)], exp_sem.at[0])
    bytes_of(fy_part, fy_sem.at[0])
    bytes_of(fy_half, fy_sem.at[2])
    bytes_of(fx_eighth, fx_sem.at[0])
    bytes_of(fx_half, fx_sem.at[2])
    bytes_of(fx_v.at[0], fx_sem.at[4])


def body(whitened, factor_x, factor_y, factor_t, mark_loadings, mark_offsets, exposure, counts):
    back = pl.pallas_call(
        kernel,
        out_shape=jax.ShapeDtypeStruct((2, 32, 1024), F32),
        in_specs=[pl.BlockSpec(memory_space=pltpu.HBM)] * 8,
        out_specs=pl.BlockSpec(memory_space=pltpu.VMEM),
        scratch_shapes=[
            pltpu.SMEM((2, MARKS), F32),
            pltpu.SMEM((MARKS,), F32),
            pltpu.SMEM((MARKS,), F32),
            pltpu.VMEM((2, 32, 1024), F32),
            pltpu.VMEM((32, 1024), F32),
            pltpu.VMEM((MARKS, 32, 1024), jnp.int32),
            pltpu.VMEM((2, 32, 1024), F32),
            pltpu.VMEM((64, 64), F32),
            pltpu.VMEM((2, N, 4, 8, 256), F32),
            pltpu.VMEM((2, 512, 512), BF16),
            pltpu.VMEM((2, 2, HALF, 512), BF16),
            pltpu.VMEM((4, 2, 2, 16, 256), F32),
            pltpu.VMEM((2, 256, 256), BF16),
            pltpu.VMEM((ROWS, 128), F32),
            pltpu.VMEM((2, HALF, 128), F32),
            pltpu.VMEM((7, ROWS, 128), F32),
            pltpu.VMEM((7, ROWS, 128), F32),
            pltpu.VMEM((256, 128), F32),
            pltpu.VMEM((256, 128), F32),
            pltpu.SemaphoreType.DMA((8,)),
            pltpu.SemaphoreType.DMA((6, 2)),
            pltpu.SemaphoreType.DMA((6, 2)),
            pltpu.SemaphoreType.DMA((2,)),
            pltpu.SemaphoreType.DMA((2,)),
            pltpu.SemaphoreType.DMA((6,)),
            pltpu.SemaphoreType.DMA((4,)),
        ],
        compiler_params=pltpu.CompilerParams(
            collective_id=0, has_side_effects=True, vmem_limit_bytes=60 * 1024 * 1024
        ),
    )(mark_loadings, mark_offsets, whitened, factor_x, factor_y, factor_t, exposure, counts)
    return back - whitened


def solution(mesh):
    placed = (
        P(None, "gx", ("gy", "ta")),
        P("gx", None),
        P(("gy", "ta"), None),
        P(),
        P(),
        P(),
        P("gx", ("gy", "ta")),
        P(None, "gx", ("gy", "ta")),
    )
    return jax.shard_map(
        body, mesh=mesh, in_specs=placed, out_specs=P(None, "gx", ("gy", "ta")), check_vma=False
    )
```

```python
import math

import jax
import jax.numpy as jnp
from jax import lax
from jax.experimental import pallas as pl
from jax.experimental.pallas import tpu as pltpu
from jax.sharding import PartitionSpec as P

MESH = pl.DeviceIdType.MESH
F32 = jnp.float32
BF16 = jnp.bfloat16
LOG2E = math.log2(math.e)
N = 16
PIECE = 16
HALF = N * PIECE
ROWS = 2 * HALF
MARKS = 64
SHIFT = 8.0
GROUP = 64
Y_IN, Y_OUT, X_IN, X_OUT, BY_IN, BY_OUT, SUMS = range(7)
X_STEPS = sorted(
    [(z, x) for z in range(8) for x in range(2) if z or x], key=lambda s: -(min(s[0], 8 - s[0]) + 2 * s[1])
)
Y_STEPS = sorted(
    [(y, c, x) for y in range(4) for c in range(2) for x in range(2) if y or c or x],
    key=lambda s: -(min(s[0], 4 - s[0]) + s[2]),
)


def split(a):
    high = a.astype(BF16)
    return high, (a - high.astype(F32)).astype(BF16)


def dot(a, b, dims=((1,), (0,))):
    def one(left, right):
        return lax.dot_general(left, right, (dims, ((), ())), preferred_element_type=F32)

    return one(a[0], b[0]) + (one(a[0], b[1]) + one(a[1], b[0]))


def dot_wide(a, b):
    both = jnp.dot(a[0], jnp.concatenate([b[0], b[1]], axis=1), preferred_element_type=F32)
    return both[:, :128] + (both[:, 128:] + jnp.dot(a[1], b[0], preferred_element_type=F32))


def swap_halves(a):
    return pltpu.roll(a, 64, 1)


def kernel(
    load_hbm, off_hbm, w_hbm, fx_hbm, fy_hbm, ft_hbm, exp_hbm, counts_hbm, out_ref,
    load_ref, off_ref, rate_off, w_v, exp_v, counts_v, sums_v, ft_v,
    fx_v, fx_parts, fxt_parts, fy_v, fyt_parts,
    t_v, field_v, send_v, recv_v, exp_send, exp_recv,
    local_sem, send_sem, recv_sem, sums_sem, exp_sem, fx_sem, fy_sem,
):
    gx = lax.axis_index("gx")
    gy = lax.axis_index("gy")
    ta = lax.axis_index("ta")
    j = gy * 2 + ta
    core = lax.rem(gy, 2)
    row = gy // 2

    def x_peer(step):
        x = gx // 8
        k = (x + step[1] - 2 * x * step[1]) * 8 + lax.rem(gx + step[0], 8)
        return k, {"gx": k}

    def y_peer(step):
        y = lax.rem(gy // 2 + step[0], 4)
        a = y * 2 + (core + step[1] - 2 * core * step[1])
        b = ta + step[2] - 2 * ta * step[2]
        return a * 2 + b, {"gy": a, "ta": b}

    x_peers = [x_peer(step) for step in X_STEPS]
    y_peers = [y_peer(step) for step in Y_STEPS]

    barrier = pltpu.get_barrier_semaphore()
    for _, at in x_peers + y_peers:
        pl.semaphore_signal(barrier, inc=1, device_id=at, device_id_type=MESH)

    loads = []
    for number, (source, target) in enumerate(
        (
            (w_hbm, w_v),
            (ft_hbm, ft_v),
            (fy_hbm, fy_v.at[row, core, ta]),
            (
                fx_hbm.at[pl.ds(pl.multiple_of(row * 8, 8), 8), pl.ds(pl.multiple_of(core * 256, 256), 256)],
                fx_v.at[core, gx, row],
            ),
            (load_hbm, load_ref),
            (off_hbm, off_ref),
            (exp_hbm, exp_v),
            (counts_hbm, counts_v),
        )
    ):
        loads.append(pltpu.make_async_copy(source, target, local_sem.at[number]))
        loads[-1].start()

    def push(source, target, sends, receives, at):
        pltpu.make_async_remote_copy(
            src_ref=source, dst_ref=target, send_sem=sends, recv_sem=receives, device_id=at, device_id_type=MESH
        ).start()

    def rows_of(k, piece, base=0):
        return pl.ds(pl.multiple_of(base + k * piece, piece), piece)

    def exchange(phase, half, me, peers, load=None):
        mine = rows_of(me, PIECE, half * HALF)
        for k, at in peers:
            rows = rows_of(k, PIECE, half * HALF)
            if load is not None:
                send_v[phase, rows, :] = load(k)
            push(send_v.at[phase, rows], recv_v.at[phase, mine], send_sem.at[phase, half], recv_sem.at[phase, half], at)
        recv_v[phase, mine, :] = send_v[phase, mine, :] if load is None else load(me)

    def bytes_of(part, sem):
        pltpu.make_async_copy(part, part, sem).wait()

    def arrived(phase, half):
        bytes_of(recv_v.at[phase, pl.ds(0, HALF - PIECE)], recv_sem.at[phase, half])

    def sent(phase, half):
        bytes_of(send_v.at[phase, pl.ds(0, HALF - PIECE)], send_sem.at[phase, half])

    def low(rows):
        return lax.broadcasted_iota(jnp.int32, (rows, 128), 1) < 64

    def pack(first, second):
        half = low(first.shape[0])
        return jnp.where(half, first, swap_halves(second)), jnp.where(half, swap_halves(first), second)

    def lines(ref):
        found = []
        for g in range(8):
            found += pack(ref[0, :, g * 128 : g * 128 + 128], ref[1, :, g * 128 : g * 128 + 128])
        return jnp.concatenate(found, axis=0)

    def turn(load, phase, half):
        for n in range(N):
            send_v[phase, pl.ds(half * HALF + n * N, N), :] = load(n)

    def y_mix(source, target, half, matrix):
        rows = pl.ds(half * HALF, HALF)
        send_v[target, rows, :] = dot_wide(matrix, split(recv_v[source, rows, :]))

    def sum_counts():
        for xt in range(4):
            xs = slice(xt * 8, xt * 8 + 8)

            def mark(m, total):
                tile = counts_v[m, xs, :].astype(F32)
                return total[0] + load_ref[0, m] * tile, total[1] + load_ref[1, m] * tile

            zero = jnp.zeros((8, 1024), F32)
            sums_v[0, xs, :], sums_v[1, xs, :] = lax.fori_loop(0, MARKS, mark, (zero, zero), unroll=4)

    for number in range(4):
        loads[number].wait()
    nothing = jnp.zeros((64, 64), F32)
    time = split(
        jnp.concatenate(
            [jnp.concatenate([ft_v[...], nothing], axis=1), jnp.concatenate([nothing, ft_v[...]], axis=1)], axis=0
        )
    )
    t_v[...] = dot(split(lines(w_v)), time, ((1,), (1,)))
    for half in range(2):
        turn(lambda n: t_v[pl.ds(half * N + n, N, stride=32), :], Y_IN, half)

    pl.semaphore_wait(barrier, 2 * (N - 1))

    mine = fy_v.at[row, core, ta]
    for step, (_, at) in zip(Y_STEPS, y_peers):
        if step[1] == 0:
            push(mine, mine, fy_sem.at[0], fy_sem.at[1], at)
    for half in range(2):
        exchange(Y_IN, half, j, y_peers)
    for number in range(4, 8):
        loads[number].wait()
    for g in range(8):
        cols = slice(g * 128, g * 128 + 128)
        even, odd = pack(exp_v[0:16, cols], exp_v[16:32, cols])
        exp_send[g * 32 : g * 32 + 16, :] = even
        exp_send[g * 32 + 16 : g * 32 + 32, :] = odd
    sum_counts()

    for _, at in x_peers[::-1]:
        push(fx_v.at[core, gx, row], fx_v.at[core, gx, row], fx_sem.at[0], fx_sem.at[1], at)
    for k, at in x_peers[::-1]:
        push(exp_send.at[rows_of(k, PIECE)], exp_recv.at[rows_of(gx, PIECE)], exp_sem.at[0], exp_sem.at[1], at)
    exp_recv[rows_of(gx, PIECE), :] = exp_send[rows_of(gx, PIECE), :]

    def scale_offset(m, carry):
        rate_off[m] = off_ref[m] * LOG2E - SHIFT
        return carry

    lax.fori_loop(0, MARKS, scale_offset, 0)
    send_v[SUMS] = lines(sums_v)
    other = {"gy": gy + 1 - 2 * core}
    fy_half = fy_v.at[:, core]
    fy_part = recv_v.at[Y_IN, pl.ds(0, 7 * 32)]
    bytes_of(fy_part, fy_sem.at[1])
    push(fy_half, fy_half, fy_sem.at[2], fy_sem.at[3], other)
    bytes_of(fy_half, fy_sem.at[3])
    fy = fy_v[...].reshape(256, 256)
    fy_parts = split(fy)
    for half in range(2):
        arrived(Y_IN, half)
        y_mix(Y_IN, Y_OUT, half, fy_parts)
        exchange(Y_OUT, half, j, y_peers)
        if half == 0:
            for k, at in x_peers[::-1]:
                push(send_v.at[SUMS, rows_of(k, 32)], recv_v.at[SUMS, rows_of(gx, 32)], sums_sem.at[0], sums_sem.at[1], at)
            recv_v[SUMS, rows_of(gx, 32), :] = send_v[SUMS, rows_of(gx, 32), :]

    fx_eighth = fx_v.at[0, pl.ds(0, N - 1), 0]
    bytes_of(fx_eighth, fx_sem.at[1])
    for step in (2, 1, 3):
        at = {"gy": lax.rem(row + step, 4) * 2 + core}
        push(fx_v.at[core, :, row], fx_v.at[core, :, row], fx_sem.at[2], fx_sem.at[3], at)
    fyt_parts[0], fyt_parts[1] = split(jnp.transpose(fy))
    for half in range(2):
        arrived(Y_OUT, half)
        turn(lambda n: recv_v[Y_OUT, pl.ds(half * HALF + n, N, stride=N), :], X_IN, half)
        exchange(X_IN, half, gx, x_peers)

    fx_half = fx_v.at[0, :, pl.ds(0, 3)]
    bytes_of(fx_half, fx_sem.at[3])
    push(fx_v.at[core], fx_v.at[core], fx_sem.at[4], fx_sem.at[5], other)
    bytes_of(fx_v.at[0], fx_sem.at[5])
    fx = jnp.concatenate([fx_v[0].reshape(ROWS, 256), fx_v[1].reshape(ROWS, 256)], axis=1)
    fx_parts[0], fx_parts[1] = split(fx)
    turned = split(jnp.transpose(fx))
    for part in range(2):
        for half in range(2):
            for k in range(N):
                x = k * 32 + half * 16
                fxt_parts[part, half, k * 16 : k * 16 + 16, :] = turned[part][x : x + 16, :]

    for half in range(2):
        arrived(X_IN, half)
    gathered = jnp.concatenate(
        [recv_v[X_IN, pl.ds(half * HALF + k * PIECE, PIECE), :] for k in range(N) for half in range(2)], axis=0
    )
    field = dot_wide((fx_parts[0], fx_parts[1]), split(gathered)) * LOG2E
    for k in range(N):
        first, second = pack(field[k * 32 : k * 32 + 16], field[k * 32 + 16 : k * 32 + 32])
        field_v[0, k * 16 : k * 16 + 16, :] = first
        field_v[1, k * 16 : k * 16 + 16, :] = second
    sums_part = recv_v.at[SUMS, pl.ds(0, ROWS - 32)]
    bytes_of(exp_recv.at[pl.ds(0, (N - 1) * 16)], exp_sem.at[1])
    bytes_of(sums_part, sums_sem.at[1])

    for begin in range(0, HALF, GROUP):
        rows = slice(begin, begin + GROUP)
        f0 = field_v[0, rows, :]
        f1 = field_v[1, rows, :]

        def mark(m, total):
            l0 = load_ref[0, m]
            l1 = load_ref[1, m]
            rate = jnp.exp2(l0 * f0 + (l1 * f1 + rate_off[m]))
            return total[0] + l0 * rate, total[1] + l1 * rate

        zero = jnp.zeros((GROUP, 128), F32)
        field_v[0, rows, :], field_v[1, rows, :] = lax.fori_loop(0, MARKS, mark, (zero, zero), unroll=16)

    residual = []
    for k in range(N):
        rows = slice(k * 16, k * 16 + 16)
        scale = exp_recv[rows, :] * (2.0**SHIFT)
        residual += pack(scale * field_v[0, rows, :], scale * field_v[1, rows, :])
    back = split(recv_v[SUMS] - jnp.concatenate(residual, axis=0))
    for half in range(2):
        send_v[X_OUT, pl.ds(half * HALF, HALF), :] = dot_wide((fxt_parts[0, half], fxt_parts[1, half]), back)
        exchange(X_OUT, half, gx, x_peers)
    for half in range(2):
        arrived(X_OUT, half)
        exchange(BY_IN, half, j, y_peers, lambda n: recv_v[X_OUT, pl.ds(half * HALF + n, N, stride=N), :])
    for half in range(2):
        arrived(BY_IN, half)
        y_mix(BY_IN, BY_OUT, half, (fyt_parts[0], fyt_parts[1]))
        exchange(BY_OUT, half, j, y_peers)
    for half in range(2):
        arrived(BY_OUT, half)
        xs = slice(half * 16, half * 16 + 16)
        rows = pl.ds(half * HALF, HALF)
        t_v[rows, :] = dot(split(recv_v[BY_OUT, rows, :]), time)
        for g in range(8):
            cols = slice(g * 128, g * 128 + 128)
            out_ref[0, xs, cols], out_ref[1, xs, cols] = pack(
                t_v[pl.ds(half * HALF + 2 * g, N, stride=N), :],
                t_v[pl.ds(half * HALF + 2 * g + 1, N, stride=N), :],
            )

    for phase in range(6):
        for half in range(2):
            sent(phase, half)
    bytes_of(sums_part, sums_sem.at[0])
    bytes_of(exp_send.at[pl.ds(0, (N - 1) * 16)], exp_sem.at[0])
    bytes_of(fy_part, fy_sem.at[0])
    bytes_of(fy_half, fy_sem.at[2])
    bytes_of(fx_eighth, fx_sem.at[0])
    bytes_of(fx_half, fx_sem.at[2])
    bytes_of(fx_v.at[0], fx_sem.at[4])


def body(whitened, factor_x, factor_y, factor_t, mark_loadings, mark_offsets, exposure, counts):
    back = pl.pallas_call(
        kernel,
        out_shape=jax.ShapeDtypeStruct((2, 32, 1024), F32),
        in_specs=[pl.BlockSpec(memory_space=pltpu.HBM)] * 8,
        out_specs=pl.BlockSpec(memory_space=pltpu.VMEM),
        scratch_shapes=[
            pltpu.SMEM((2, MARKS), F32),
            pltpu.SMEM((MARKS,), F32),
            pltpu.SMEM((MARKS,), F32),
            pltpu.VMEM((2, 32, 1024), F32),
            pltpu.VMEM((32, 1024), F32),
            pltpu.VMEM((MARKS, 32, 1024), jnp.int32),
            pltpu.VMEM((2, 32, 1024), F32),
            pltpu.VMEM((64, 64), F32),
            pltpu.VMEM((2, N, 4, 8, 256), F32),
            pltpu.VMEM((2, 512, 512), BF16),
            pltpu.VMEM((2, 2, HALF, 512), BF16),
            pltpu.VMEM((4, 2, 2, 16, 256), F32),
            pltpu.VMEM((2, 256, 256), BF16),
            pltpu.VMEM((ROWS, 128), F32),
            pltpu.VMEM((2, HALF, 128), F32),
            pltpu.VMEM((7, ROWS, 128), F32),
            pltpu.VMEM((7, ROWS, 128), F32),
            pltpu.VMEM((256, 128), F32),
            pltpu.VMEM((256, 128), F32),
            pltpu.SemaphoreType.DMA((8,)),
            pltpu.SemaphoreType.DMA((6, 2)),
            pltpu.SemaphoreType.DMA((6, 2)),
            pltpu.SemaphoreType.DMA((2,)),
            pltpu.SemaphoreType.DMA((2,)),
            pltpu.SemaphoreType.DMA((6,)),
            pltpu.SemaphoreType.DMA((4,)),
        ],
        compiler_params=pltpu.CompilerParams(
            collective_id=0, has_side_effects=True, vmem_limit_bytes=60 * 1024 * 1024
        ),
    )(mark_loadings, mark_offsets, whitened, factor_x, factor_y, factor_t, exposure, counts)
    return back - whitened


def solution(mesh):
    placed = (
        P(None, "gx", ("gy", "ta")),
        P("gx", None),
        P(("gy", "ta"), None),
        P(),
        P(),
        P(),
        P("gx", ("gy", "ta")),
        P(None, "gx", ("gy", "ta")),
    )
    return jax.shard_map(
        body, mesh=mesh, in_specs=placed, out_specs=P(None, "gx", ("gy", "ta")), check_vma=False
    )
```
